32 devices in a mesh: band: 4 (over y, core), grid: 8 (over z, x).
Axes of the slice: x: 2, y: 2, z: 4, core: 2. Of those that a mesh axis runs over, the one named last changes fastest.
Arguments:
- ground: float32 [4, 128, 128, 128], P('band', 'grid'), may hold values from -6 to 6
- response: float32 [4, 2, 2, 128, 128, 128], P('band', None, None, None, 'grid'), may hold values from -0.6 to 0.6
- kernel_xc: float32 [128, 128, 128], P('grid'), may hold values from -2 to -0.3
Outputs:
- applied: float32 [4, 2, 2, 128, 128, 128], P('band', None, None, None, 'grid')
The draws below stay inside these ranges and needn't reach their ends.
All inputs are finite; a program needn't handle non-finite values.
Results may differ from the reference program's by a relative error of at most 0.0001.
Values sent between devices are 32-bit elements; how exact they have to be, the bound alone decides.
A program may use at most 64 MiB of HBM per device.

```python
import math
import jax
import jax.numpy as jnp
from jax import lax

NG = 128
BANDS = 4


def block_levels(rng, dims, pieces, smallest, high):
    def one(position, parts):
        heights = jax.random.uniform(jax.random.fold_in(jax.random.fold_in(rng, 6), position), (parts,), jnp.float32, smallest / len(pieces), high / len(pieces))
        return jnp.repeat(jnp.exp(heights), dims[position] // parts).reshape((-1,) + (1,) * (len(dims) - position - 1))

    loudness = one(*pieces[0])
    for cut in pieces[1:]:
        loudness = loudness * one(*cut)
    return loudness


def noise(own_key, shape, deviation, reach, cuts=(), dtype=jnp.bfloat16):
    values = jax.random.normal(own_key, shape, jnp.float32) * deviation
    if len(cuts) > 0:
        values = block_levels(own_key, shape, cuts, -0.22, 0.18) * values
    return jnp.clip(values, min=-reach, max=reach).astype(dtype)


def setup_inputs(seed: int = 0) -> dict:
    splits = jax.random.split(jax.random.key(seed), 4)
    return {
        "ground": noise(splits[0], (BANDS, NG, NG, NG), 1.0, 6.0, ((0, 4), (1, 8)), jnp.float32),
        "response": noise(splits[1], (BANDS, 2, 2, NG, NG, NG), 0.1, 0.6, ((0, 4), (4, 8)), jnp.float32),
        "kernel_xc": jnp.clip(-2.0 + 1.7 * jax.random.uniform(splits[2], (NG, NG, NG), jnp.float32) ** block_levels(splits[2], (NG, NG, NG), ((0, 8),), -0.2, 0.2), -2.0, -0.3),
    }


spacing = 0.4527


def signed_freq(length):
    positions = jnp.arange(length)
    return jnp.where(positions < (length + 1) // 2, positions, positions - length).astype(jnp.float32)


def coulomb_table(length):
    freqs = signed_freq(length)
    squares = freqs[:, None, None] ** 2 + freqs[None, :, None] ** 2 + freqs[None, None, :] ** 2
    edge_len = spacing * length
    return jnp.where(squares > 0.5, edge_len * edge_len / (math.pi * jnp.maximum(squares, 1.0)), 0.0)


def reference(ground, response, kernel_xc):
    zero_field = jnp.zeros(ground.shape[1:], jnp.float32)

    def accumulate(carry, inputs):
        orbital, coeffs = inputs
        plus = jnp.fft.ifftn(coeffs[0, 0] + 1j * coeffs[0, 1], norm="ortho")
        minus = jnp.fft.ifftn(coeffs[1, 0] + 1j * coeffs[1, 1], norm="ortho")
        term = orbital * (plus + jnp.conj(minus))
        return (carry[0] + jnp.real(term), carry[1] + jnp.imag(term)), None

    (dens_real, dens_imag), _ = lax.scan(accumulate, (zero_field, zero_field), (ground, response))
    density = dens_real + 1j * dens_imag
    hartree = jnp.fft.ifftn(coulomb_table(NG) * jnp.fft.fftn(density, norm="ortho"), norm="ortho")
    potential = hartree + kernel_xc * density

    def apply_one(orbital):
        plus = jnp.fft.fftn(potential * orbital, norm="ortho")
        minus = jnp.fft.fftn(jnp.conj(potential) * orbital, norm="ortho")
        return jnp.stack((jnp.stack((jnp.real(plus), jnp.imag(plus))), jnp.stack((jnp.real(minus), jnp.imag(minus))))).astype(jnp.float32)

    return lax.map(apply_one, ground)
```

```python
import math

import jax
import jax.numpy as jnp
import numpy as np
from jax import lax
from jax.sharding import PartitionSpec as P

high = lax.Precision.HIGH
spacing = 0.4527


def dft_pair(length, direction, rows=None, columns=None):
    rows = np.arange(length) if rows is None else rows
    columns = np.arange(length) if columns is None else columns
    angles = (rows[:, None] * columns[None, :] % length) * (2.0 * math.pi / length)
    cosine = np.cos(angles) / math.sqrt(length)
    sine = direction * np.sin(angles) / math.sqrt(length)
    pairs = (np.stack((cosine, sine), axis=1), np.stack((-sine, cosine), axis=1))
    return np.stack(pairs, axis=0).astype(np.float32)


def ein(form, operand, table):
    return jnp.einsum(form, operand, table, precision=high)


def signed_freq(positions, length):
    return jnp.where(positions < (length + 1) // 2, positions, positions - length).astype(
        jnp.float32
    )


def coulomb(freq_first, freq_second, freq_third, length):
    squares = (
        freq_first[:, None, None] ** 2
        + freq_second[None, :, None] ** 2
        + freq_third[None, None, :] ** 2
    )
    edge_len = spacing * length
    return jnp.where(
        squares > 0.5, edge_len * edge_len / (math.pi * jnp.maximum(squares, 1.0)), 0.0
    )


def swap(values, bit, size):
    return lax.ppermute(values, "band", [(i, i ^ bit) for i in range(size)])


def hartree(density, axes, device, devices, numbers):
    length = density.shape[-1]
    forward, backward = dft_pair(length, -1.0), dft_pair(length, 1.0)
    wave = ein("cxyz,cydk->dxkz", density, forward)
    wave = ein("dxkz,dzem->exkm", wave, forward)
    wave = lax.all_to_all(wave, axes, split_axis=2, concat_axis=1, tiled=True)
    rows = length // devices
    mine = device * rows + jnp.arange(rows, dtype=jnp.int32)
    freqs = signed_freq(jnp.arange(length, dtype=jnp.int32), length)
    weights = coulomb(freqs, signed_freq(mine, length), freqs, length)
    wave = ein("cxyz,cxdk->dkyz", wave, dft_pair(length, -1.0, rows=numbers)) * weights
    wave = ein("dkyz,dkex->exyz", wave, dft_pair(length, 1.0, columns=numbers))
    wave = lax.all_to_all(wave, axes, split_axis=1, concat_axis=2, tiled=True)
    cell = ein("dxkz,dzem->exkm", wave, backward)
    return ein("cxyz,cydk->dxkz", cell, backward)


def on_device(bands, grids, ground, response, kernel_xc):
    grid_len = ground.shape[2]
    planes = ground.shape[1]
    forward = dft_pair(grid_len, -1.0)
    backward = dft_pair(grid_len, 1.0)
    orbital = ground[0]

    flip = np.array([1.0, -1.0], np.float32)[None, None, :, None]
    partial = None
    for harmonic in range(2):
        table = backward if harmonic == 0 else backward * flip
        wave = ein("cxyz,cxdk->dkyz", response[0, harmonic], backward)
        wave = lax.all_to_all(wave, "grid", split_axis=1, concat_axis=2, tiled=True)
        wave = ein("dxkz,dzem->exkm", wave, backward)
        cell = ein("cxyz,cydk->dxkz", wave, table)
        partial = cell if partial is None else partial + cell
    partial = partial * orbital

    me_band = lax.axis_index("band")
    if planes % bands == 0 and bands & (bands - 1) == 0:
        dens = partial
        kernel = kernel_xc
        bit = bands // 2
        bits = []
        while bit >= 1:
            bits.append(bit)
            bit //= 2
        steps = list(reversed(bits))
        low = jnp.int32(0)
        for bit in steps:
            half = dens.shape[1] // 2
            mine = (me_band // bit) % 2
            keep = lax.dynamic_slice_in_dim(dens, mine * half, half, 1)
            give = lax.dynamic_slice_in_dim(dens, (1 - mine) * half, half, 1)
            dens = keep + swap(give, bit, bands)
            low = low + mine * half
        own = dens.shape[1]
        kernel = lax.dynamic_slice_in_dim(kernel_xc, low, own, 0)
        place = [0] * bands
        for b in range(bands):
            size = planes
            for bit in steps:
                size //= 2
                place[b] += ((b // bit) % 2) * (size // own)
        numbers = (
            np.arange(grids)[None, :, None] * planes
            + np.array(place)[:, None, None] * own
            + np.arange(own)[None, None, :]
        ).reshape(-1)
        device = me_band * grids + lax.axis_index("grid")
        pot = hartree(dens, ("band", "grid"), device, bands * grids, numbers)
        pot = pot + kernel * dens
        for bit in reversed(steps):
            mine = (me_band // bit) % 2
            other = swap(pot, bit, bands)
            first = jnp.where(mine == 0, pot, other)
            second = jnp.where(mine == 0, other, pot)
            pot = jnp.concatenate((first, second), axis=1)
    else:
        dens = lax.psum(partial, "band")
        pot = hartree(dens, "grid", lax.axis_index("grid"), grids, None)
        pot = pot + kernel_xc * dens

    prod = pot * orbital
    outs = []
    for harmonic in range(2):
        table = forward if harmonic == 0 else forward * flip.reshape(2, 1, 1, 1)
        wave = ein("cxyz,cydk->dxkz", prod, table)
        wave = ein("dxkz,dzem->exkm", wave, forward)
        wave = lax.all_to_all(wave, "grid", split_axis=2, concat_axis=1, tiled=True)
        outs.append(ein("cxyz,cxdk->dkyz", wave, forward))
    return jnp.stack(outs, axis=0)[None]


def solution(mesh):
    bands, grids = mesh.shape["band"], mesh.shape["grid"]

    def body(ground, response, kernel_xc):
        return on_device(bands, grids, ground, response, kernel_xc)

    return jax.shard_map(
        body,
        mesh=mesh,
        in_specs=(
            P("band", "grid", None, None),
            P("band", None, None, None, "grid", None),
            P("grid", None, None),
        ),
        out_specs=P("band", None, None, None, "grid", None),
        check_vma=False,
    )
```

```python
import functools
import math

import jax
import jax.numpy as jnp
import ml_dtypes
import numpy as np
from jax import lax
from jax.experimental import pallas as pl
from jax.experimental.pallas import tpu as pltpu
from jax.sharding import PartitionSpec as P

high = lax.Precision.HIGH
spacing = 0.4527


def dft_pair(length, direction, rows=None, columns=None):
    rows = np.arange(length) if rows is None else rows
    columns = np.arange(length) if columns is None else columns
    angles = (rows[:, None] * columns[None, :] % length) * (2.0 * math.pi / length)
    cosine = np.cos(angles) / math.sqrt(length)
    sine = direction * np.sin(angles) / math.sqrt(length)
    pairs = (np.stack((cosine, sine), axis=1), np.stack((-sine, cosine), axis=1))
    return np.stack(pairs, axis=0).astype(np.float32)


def halves(values):
    upper = values.astype(jnp.bfloat16)
    return upper, (values - upper.astype(jnp.float32)).astype(jnp.bfloat16)


def table_halves(table):
    values = table.reshape(2 * table.shape[1], -1)
    upper = values.astype(ml_dtypes.bfloat16)
    lower = (values - upper.astype(np.float32)).astype(ml_dtypes.bfloat16)
    return np.stack((upper, lower))


def dot(first, second):
    return jnp.dot(first, second, preferred_element_type=jnp.float32)


def times_table(values, table):
    upper, lower = halves(values)
    return dot(upper, table[0]) + (dot(upper, table[1]) + dot(lower, table[0]))


def table_times(table, values):
    upper, lower = halves(values)
    return dot(table[0], upper) + (dot(table[1], upper) + dot(table[0], lower))


def meet(group, devices):
    me = lax.axis_index(group)
    barrier = pltpu.get_barrier_semaphore()
    for step in range(1, devices):
        peer = lax.rem(me + step, devices)
        pl.semaphore_signal(
            barrier, inc=1, device_id={group: peer}, device_id_type=pl.DeviceIdType.MESH
        )
    pl.semaphore_wait(barrier, devices - 1)
    return me


def arrive_kernel(grids, resp, orbital, left_x, right_z, left_y, out, away, here, sent, got, own):
    rows, length = orbital.shape[0], orbital.shape[1]
    block = rows * rows
    me = meet("grid", grids)
    copies = []
    for harmonic in range(2):

        def transform_x(pair, carry):
            column = []
            for k in range(2):
                picked = pl.ds(2 * pair + k, length, stride=rows)
                column.append(
                    jnp.concatenate([resp[harmonic, c, picked, :] for c in range(2)], axis=0)
                )
            wave = table_times(left_x, jnp.concatenate(column, axis=1))
            for k in range(2):
                picked = pl.ds(2 * pair + k, length, stride=rows)
                for c in range(2):
                    away[harmonic, c, picked, :] = wave[
                        c * length : (c + 1) * length, k * length : (k + 1) * length
                    ]
            return carry

        lax.fori_loop(0, rows // 2, transform_x, 0)
        mine = pltpu.make_async_copy(
            away.at[harmonic, :, pl.ds(pl.multiple_of(me * block, block), block), :],
            here.at[harmonic, me],
            own.at[harmonic],
        )
        mine.start()
        steps = []
        for step in range(1, grids):
            peer = lax.rem(me + step, grids)
            copy = pltpu.make_async_remote_copy(
                src_ref=away.at[
                    harmonic, :, pl.ds(pl.multiple_of(peer * block, block), block), :
                ],
                dst_ref=here.at[harmonic, me],
                send_sem=sent.at[harmonic, step],
                recv_sem=got.at[harmonic, step],
                device_id={"grid": peer},
                device_id_type=pl.DeviceIdType.MESH,
            )
            copy.start()
            steps.append(copy)
        copies.append((mine, steps))
    for harmonic in range(2):
        mine, steps = copies[harmonic]
        mine.wait()
        for copy in steps:
            copy.wait_recv()

        def transform_zy(pair, carry):
            lines = []
            for k in range(2):
                at = pl.ds(pl.multiple_of((2 * pair + k) * rows, rows), rows)
                lines.append(
                    jnp.concatenate(
                        [
                            jnp.concatenate(
                                [here[harmonic, s, c, at, :] for s in range(grids)], axis=0
                            )
                            for c in range(2)
                        ],
                        axis=1,
                    )
                )
            wave = times_table(jnp.concatenate(lines, axis=0), right_z)
            planes = []
            for k in range(2):
                line = wave[k * length : (k + 1) * length]
                planes.append(
                    jnp.concatenate([line[:, :length], line[:, length:]], axis=0)
                )
            cell = table_times(left_y.at[harmonic], jnp.concatenate(planes, axis=1))
            for k in range(2):
                plane = 2 * pair + k
                for c in range(2):
                    value = cell[c * length : (c + 1) * length, k * length : (k + 1) * length]
                    if harmonic == 0:
                        out[c, plane] = value
                    else:
                        out[c, plane] = (out[c, plane] + value) * orbital[plane]
            return carry

        lax.fori_loop(0, rows // 2, transform_zy, 0)
    for mine, steps in copies:
        for copy in steps:
            copy.wait_send()


def leave_kernel(grids, pot, orbital, left_y, right_z, left_x, out, away, here, sent, got, own):
    rows, length = orbital.shape[0], orbital.shape[1]
    block = rows * rows
    me = meet("grid", grids)
    copies = []
    for harmonic in range(2):

        def transform_yz(pair, carry):
            planes = []
            for k in range(2):
                plane = 2 * pair + k
                weight = orbital[plane]
                planes.append(
                    jnp.concatenate([pot[c, plane] * weight for c in range(2)], axis=0)
                )
            wave = table_times(left_y.at[harmonic], jnp.concatenate(planes, axis=1))
            lines = []
            for k in range(2):
                part = wave[:, k * length : (k + 1) * length]
                lines.append(jnp.concatenate([part[:length], part[length:]], axis=1))
            wave = times_table(jnp.concatenate(lines, axis=0), right_z)
            for k in range(2):
                at = pl.ds(pl.multiple_of((2 * pair + k) * rows, rows), rows)
                for s in range(grids):
                    first = k * length + s * rows
                    for c in range(2):
                        away[harmonic, s, c, at, :] = wave[
                            first : first + rows, c * length : (c + 1) * length
                        ]
            return carry

        lax.fori_loop(0, rows // 2, transform_yz, 0)
        at_me = pl.ds(pl.multiple_of(me * block, block), block)
        mine = pltpu.make_async_copy(
            away.at[harmonic, me], here.at[harmonic, :, at_me, :], own.at[harmonic]
        )
        mine.start()
        steps = []
        for step in range(1, grids):
            peer = lax.rem(me + step, grids)
            copy = pltpu.make_async_remote_copy(
                src_ref=away.at[harmonic, peer],
                dst_ref=here.at[harmonic, :, at_me, :],
                send_sem=sent.at[harmonic, step],
                recv_sem=got.at[harmonic, step],
                device_id={"grid": peer},
                device_id_type=pl.DeviceIdType.MESH,
            )
            copy.start()
            steps.append(copy)
        copies.append((mine, steps))
    for harmonic in range(2):
        mine, steps = copies[harmonic]
        mine.wait()
        for copy in steps:
            copy.wait_recv()

        def transform_x(pair, carry):
            column = []
            for k in range(2):
                picked = pl.ds(2 * pair + k, length, stride=rows)
                column.append(
                    jnp.concatenate([here[harmonic, c, picked, :] for c in range(2)], axis=0)
                )
            wave = table_times(left_x, jnp.concatenate(column, axis=1))
            for k in range(2):
                picked = pl.ds(2 * pair + k, length, stride=rows)
                for c in range(2):
                    out[harmonic, c, picked, :] = wave[
                        c * length : (c + 1) * length, k * length : (k + 1) * length
                    ]
            return carry

        lax.fori_loop(0, rows // 2, transform_x, 0)
    for mine, steps in copies:
        for copy in steps:
            copy.wait_send()


def call(kernel, grids, rows, length, out_shape, by_source, collective_id, *operands):
    flat = (2, 2, length * rows, length)
    blocks = (2, grids, 2, rows * rows, length)
    return pl.pallas_call(
        functools.partial(kernel, grids),
        out_shape=jax.ShapeDtypeStruct(out_shape, jnp.float32),
        in_specs=[pl.BlockSpec(memory_space=pltpu.VMEM)] * len(operands),
        out_specs=pl.BlockSpec(memory_space=pltpu.VMEM),
        scratch_shapes=[
            pltpu.VMEM(flat if by_source else blocks, jnp.float32),
            pltpu.VMEM(blocks if by_source else flat, jnp.float32),
            pltpu.SemaphoreType.DMA((2, grids)),
            pltpu.SemaphoreType.DMA((2, grids)),
            pltpu.SemaphoreType.DMA((2,)),
        ],
        compiler_params=pltpu.CompilerParams(
            collective_id=collective_id, has_side_effects=True, vmem_limit_bytes=40 * 2**20
        ),
    )(*operands)


def ein(form, operand, table):
    return jnp.einsum(form, operand, table, precision=high)


def signed_freq(positions, length):
    return jnp.where(positions < (length + 1) // 2, positions, positions - length).astype(
        jnp.float32
    )


def coulomb(freq_first, freq_second, freq_third, length):
    squares = (
        freq_first[:, None, None] ** 2
        + freq_second[None, :, None] ** 2
        + freq_third[None, None, :] ** 2
    )
    edge_len = spacing * length
    return jnp.where(
        squares > 0.5, edge_len * edge_len / (math.pi * jnp.maximum(squares, 1.0)), 0.0
    )


def swap(values, bit, size):
    return lax.ppermute(values, "band", [(i, i ^ bit) for i in range(size)])


def hartree(density, axes, device, devices, numbers):
    length = density.shape[-1]
    forward, backward = dft_pair(length, -1.0), dft_pair(length, 1.0)
    wave = ein("cxyz,cydk->dxkz", density, forward)
    wave = ein("dxkz,dzem->exkm", wave, forward)
    wave = lax.all_to_all(wave, axes, split_axis=2, concat_axis=1, tiled=True)
    rows = length // devices
    mine = device * rows + jnp.arange(rows, dtype=jnp.int32)
    freqs = signed_freq(jnp.arange(length, dtype=jnp.int32), length)
    weights = coulomb(freqs, signed_freq(mine, length), freqs, length)
    wave = ein("cxyz,cxdk->dkyz", wave, dft_pair(length, -1.0, rows=numbers)) * weights
    wave = ein("dkyz,dkex->exyz", wave, dft_pair(length, 1.0, columns=numbers))
    wave = lax.all_to_all(wave, axes, split_axis=1, concat_axis=2, tiled=True)
    cell = ein("dxkz,dzem->exkm", wave, backward)
    return ein("cxyz,cydk->dxkz", cell, backward)


def on_device(bands, grids, ground, response, kernel_xc):
    grid_len = ground.shape[2]
    planes = ground.shape[1]
    forward = dft_pair(grid_len, -1.0)
    backward = dft_pair(grid_len, 1.0)
    orbital = ground[0]

    flip = np.array([1.0, -1.0], np.float32)
    turn = (2, 3, 0, 1)
    left_y = np.stack([
        table_halves(backward.transpose(turn)),
        table_halves((backward * flip[:, None]).transpose(turn)),
    ])
    partial = call(
        arrive_kernel, grids, planes, grid_len, (2, planes, grid_len, grid_len), True, 0,
        response.reshape(2, 2, grid_len * planes, grid_len),
        orbital,
        table_halves(backward.transpose(turn)),
        table_halves(backward),
        left_y,
    )

    me_band = lax.axis_index("band")
    if planes % bands == 0 and bands & (bands - 1) == 0:
        dens = partial
        kernel = kernel_xc
        bit = bands // 2
        bits = []
        while bit >= 1:
            bits.append(bit)
            bit //= 2
        steps = list(reversed(bits))
        low = jnp.int32(0)
        for bit in steps:
            half = dens.shape[1] // 2
            mine = (me_band // bit) % 2
            keep = lax.dynamic_slice_in_dim(dens, mine * half, half, 1)
            give = lax.dynamic_slice_in_dim(dens, (1 - mine) * half, half, 1)
            dens = keep + swap(give, bit, bands)
            low = low + mine * half
        own = dens.shape[1]
        kernel = lax.dynamic_slice_in_dim(kernel_xc, low, own, 0)
        place = [0] * bands
        for b in range(bands):
            size = planes
            for bit in steps:
                size //= 2
                place[b] += ((b // bit) % 2) * (size // own)
        numbers = (
            np.arange(grids)[None, :, None] * planes
            + np.array(place)[:, None, None] * own
            + np.arange(own)[None, None, :]
        ).reshape(-1)
        device = me_band * grids + lax.axis_index("grid")
        pot = hartree(dens, ("band", "grid"), device, bands * grids, numbers)
        pot = pot + kernel * dens
        for bit in reversed(steps):
            mine = (me_band // bit) % 2
            other = swap(pot, bit, bands)
            first = jnp.where(mine == 0, pot, other)
            second = jnp.where(mine == 0, other, pot)
            pot = jnp.concatenate((first, second), axis=1)
    else:
        dens = lax.psum(partial, "band")
        pot = hartree(dens, "grid", lax.axis_index("grid"), grids, None)
        pot = pot + kernel_xc * dens

    left_y = np.stack([
        table_halves(forward.transpose(turn)),
        table_halves((forward * flip[:, None, None, None]).transpose(turn)),
    ])
    out = call(
        leave_kernel, grids, planes, grid_len, (2, 2, grid_len * planes, grid_len), False, 1,
        pot, orbital, left_y, table_halves(forward), table_halves(forward.transpose(turn)),
    )
    return out.reshape(1, 2, 2, grid_len, planes, grid_len)


def solution(mesh):
    bands, grids = mesh.shape["band"], mesh.shape["grid"]

    def body(ground, response, kernel_xc):
        return on_device(bands, grids, ground, response, kernel_xc)

    return jax.shard_map(
        body,
        mesh=mesh,
        in_specs=(
            P("band", "grid", None, None),
            P("band", None, None, None, "grid", None),
            P("grid", None, None),
        ),
        out_specs=P("band", None, None, None, "grid", None),
        check_vma=False,
    )
```

```python
import functools
import math

import jax
import jax.numpy as jnp
import ml_dtypes
import numpy as np
from jax import lax
from jax.experimental import pallas as pl
from jax.experimental.pallas import tpu as pltpu
from jax.sharding import PartitionSpec as P

high = lax.Precision.HIGH
spacing = 0.4527


def dft_pair(length, direction, rows=None, columns=None):
    rows = np.arange(length) if rows is None else rows
    columns = np.arange(length) if columns is None else columns
    angles = (rows[:, None] * columns[None, :] % length) * (2.0 * math.pi / length)
    cosine = np.cos(angles) / math.sqrt(length)
    sine = direction * np.sin(angles) / math.sqrt(length)
    pairs = (np.stack((cosine, sine), axis=1), np.stack((-sine, cosine), axis=1))
    return np.stack(pairs, axis=0).astype(np.float32)


def halves(values):
    upper = values.astype(jnp.bfloat16)
    return upper, (values - upper.astype(jnp.float32)).astype(jnp.bfloat16)


def table_halves(table):
    values = table.reshape(2 * table.shape[1], -1)
    upper = values.astype(ml_dtypes.bfloat16)
    lower = (values - upper.astype(np.float32)).astype(ml_dtypes.bfloat16)
    return np.stack((upper, lower))


def dot(first, second):
    return jnp.dot(first, second, preferred_element_type=jnp.float32)


def times_table(values, table):
    upper, lower = halves(values)
    return dot(upper, table[0]) + (dot(upper, table[1]) + dot(lower, table[0]))


def table_times(table, values):
    upper, lower = halves(values)
    return dot(table[0], upper) + (dot(table[1], upper) + dot(table[0], lower))


def meet(group, devices):
    me = lax.axis_index(group)
    barrier = pltpu.get_barrier_semaphore()
    for step in range(1, devices):
        peer = lax.rem(me + step, devices)
        pl.semaphore_signal(
            barrier, inc=1, device_id={group: peer}, device_id_type=pl.DeviceIdType.MESH
        )
    pl.semaphore_wait(barrier, devices - 1)
    return me


def arrive_kernel(grids, resp, orbital, left_x, right_z, left_y, out, away, here, sent, got, own):
    rows, length = orbital.shape[0], orbital.shape[1]
    block = rows * rows
    me = meet("grid", grids)
    copies = []
    for harmonic in range(2):

        def transform_x(pair, carry):
            column = []
            for k in range(2):
                picked = pl.ds(2 * pair + k, length, stride=rows)
                column.append(
                    jnp.concatenate([resp[harmonic, c, picked, :] for c in range(2)], axis=0)
                )
            wave = table_times(left_x, jnp.concatenate(column, axis=1))
            for k in range(2):
                picked = pl.ds(2 * pair + k, length, stride=rows)
                for c in range(2):
                    away[harmonic, c, picked, :] = wave[
                        c * length : (c + 1) * length, k * length : (k + 1) * length
                    ]
            return carry

        lax.fori_loop(0, rows // 2, transform_x, 0)
        mine = pltpu.make_async_copy(
            away.at[harmonic, :, pl.ds(pl.multiple_of(me * block, block), block), :],
            here.at[harmonic, me],
            own.at[harmonic],
        )
        mine.start()
        steps = []
        for step in range(1, grids):
            peer = lax.rem(me + step, grids)
            copy = pltpu.make_async_remote_copy(
                src_ref=away.at[
                    harmonic, :, pl.ds(pl.multiple_of(peer * block, block), block), :
                ],
                dst_ref=here.at[harmonic, me],
                send_sem=sent.at[harmonic, step],
                recv_sem=got.at[harmonic, step],
                device_id={"grid": peer},
                device_id_type=pl.DeviceIdType.MESH,
            )
            copy.start()
            steps.append(copy)
        copies.append((mine, steps))
    for harmonic in range(2):
        mine, steps = copies[harmonic]
        mine.wait()
        for copy in steps:
            copy.wait_recv()

        def transform_zy(pair, carry):
            lines = []
            for k in range(2):
                at = pl.ds(pl.multiple_of((2 * pair + k) * rows, rows), rows)
                lines.append(
                    jnp.concatenate(
                        [
                            jnp.concatenate(
                                [here[harmonic, s, c, at, :] for s in range(grids)], axis=0
                            )
                            for c in range(2)
                        ],
                        axis=1,
                    )
                )
            wave = times_table(jnp.concatenate(lines, axis=0), right_z)
            planes = []
            for k in range(2):
                line = wave[k * length : (k + 1) * length]
                planes.append(
                    jnp.concatenate([line[:, :length], line[:, length:]], axis=0)
                )
            cell = table_times(left_y.at[harmonic], jnp.concatenate(planes, axis=1))
            for k in range(2):
                plane = 2 * pair + k
                for c in range(2):
                    value = cell[c * length : (c + 1) * length, k * length : (k + 1) * length]
                    if harmonic == 0:
                        out[c, plane] = value
                    else:
                        out[c, plane] = (out[c, plane] + value) * orbital[plane]
            return carry

        lax.fori_loop(0, rows // 2, transform_zy, 0)
    for mine, steps in copies:
        for copy in steps:
            copy.wait_send()


def leave_kernel(grids, pot, orbital, left_y, right_z, left_x, out, away, here, sent, got, own):
    rows, length = orbital.shape[0], orbital.shape[1]
    block = rows * rows
    me = meet("grid", grids)
    copies = []
    for harmonic in range(2):

        def transform_yz(pair, carry):
            planes = []
            for k in range(2):
                plane = 2 * pair + k
                weight = orbital[plane]
                planes.append(
                    jnp.concatenate([pot[c, plane] * weight for c in range(2)], axis=0)
                )
            wave = table_times(left_y.at[harmonic], jnp.concatenate(planes, axis=1))
            lines = []
            for k in range(2):
                part = wave[:, k * length : (k + 1) * length]
                lines.append(jnp.concatenate([part[:length], part[length:]], axis=1))
            wave = times_table(jnp.concatenate(lines, axis=0), right_z)
            for k in range(2):
                at = pl.ds(pl.multiple_of((2 * pair + k) * rows, rows), rows)
                for s in range(grids):
                    first = k * length + s * rows
                    for c in range(2):
                        away[harmonic, s, c, at, :] = wave[
                            first : first + rows, c * length : (c + 1) * length
                        ]
            return carry

        lax.fori_loop(0, rows // 2, transform_yz, 0)
        at_me = pl.ds(pl.multiple_of(me * block, block), block)
        mine = pltpu.make_async_copy(
            away.at[harmonic, me], here.at[harmonic, :, at_me, :], own.at[harmonic]
        )
        mine.start()
        steps = []
        for step in range(1, grids):
            peer = lax.rem(me + step, grids)
            copy = pltpu.make_async_remote_copy(
                src_ref=away.at[harmonic, peer],
                dst_ref=here.at[harmonic, :, at_me, :],
                send_sem=sent.at[harmonic, step],
                recv_sem=got.at[harmonic, step],
                device_id={"grid": peer},
                device_id_type=pl.DeviceIdType.MESH,
            )
            copy.start()
            steps.append(copy)
        copies.append((mine, steps))
    for harmonic in range(2):
        mine, steps = copies[harmonic]
        mine.wait()
        for copy in steps:
            copy.wait_recv()

        def transform_x(pair, carry):
            column = []
            for k in range(2):
                picked = pl.ds(2 * pair + k, length, stride=rows)
                column.append(
                    jnp.concatenate([here[harmonic, c, picked, :] for c in range(2)], axis=0)
                )
            wave = table_times(left_x, jnp.concatenate(column, axis=1))
            for k in range(2):
                picked = pl.ds(2 * pair + k, length, stride=rows)
                for c in range(2):
                    out[harmonic, c, picked, :] = wave[
                        c * length : (c + 1) * length, k * length : (k + 1) * length
                    ]
            return carry

        lax.fori_loop(0, rows // 2, transform_x, 0)
    for mine, steps in copies:
        for copy in steps:
            copy.wait_send()


def middle_kernel(
    grids, part, kernel, weights, front_y, right_front, front_x, back_x, back_y, right_back, out,
    got_half, half, got_own, dens, away, here, back_away, back_here, pair_sent, pair_got, sent, got,
):
    devices = 4 * grids
    planes, length = part.shape[1], part.shape[2]
    own = planes // 4
    rows = length // devices
    block = 2 * own * rows
    band, grid = lax.axis_index("band"), lax.axis_index("grid")
    me = band * grids + grid

    def at(device):
        return {"band": device // grids, "grid": lax.rem(device, grids)}

    barrier = pltpu.get_barrier_semaphore()

    def greet(step, carry):
        pl.semaphore_signal(
            barrier, inc=1, device_id=at(lax.rem(me + step, devices)),
            device_id_type=pl.DeviceIdType.MESH,
        )
        return carry

    lax.fori_loop(1, devices, greet, 0)
    pl.semaphore_wait(barrier, devices - 1)

    low_bit, high_bit = lax.rem(band, 2), band // 2
    near = {"band": 2 * high_bit + (1 - low_bit), "grid": grid}
    far = {"band": 2 * (1 - high_bit) + low_bit, "grid": grid}

    def pair_copy(source, target, place, index):
        return pltpu.make_async_remote_copy(
            src_ref=source, dst_ref=target, send_sem=pair_sent.at[index],
            recv_sem=pair_got.at[index], device_id=place, device_id_type=pl.DeviceIdType.MESH,
        )

    first = pair_copy(part.at[:, pl.ds((1 - low_bit) * 2 * own, 2 * own)], got_half, near, 0)
    first.start()
    first.wait()

    def add_half(plane, carry):
        for c in range(2):
            half[c, plane] = part[c, low_bit * 2 * own + plane] + got_half[c, plane]
        return carry

    lax.fori_loop(0, 2 * own, add_half, 0)
    second = pair_copy(half.at[:, pl.ds((1 - high_bit) * own, own)], got_own, far, 1)
    second.start()
    second.wait()

    def add_own(plane, carry):
        for c in range(2):
            dens[c, plane] = half[c, high_bit * own + plane] + got_own[c, plane]
        return carry

    lax.fori_loop(0, own, add_own, 0)

    def exchange(source, target, index):
        mine = pl.ds(pl.multiple_of(me * block, block), block)

        def copy_of(step):
            peer = lax.rem(me + step, devices)
            return pltpu.make_async_remote_copy(
                src_ref=source.at[pl.ds(pl.multiple_of(peer * block, block), block)],
                dst_ref=target.at[mine],
                send_sem=sent.at[index, step],
                recv_sem=got.at[index, step],
                device_id=at(peer),
                device_id_type=pl.DeviceIdType.MESH,
            )

        def start(step, carry):
            copy_of(step).start()
            return carry

        def finish(step, carry):
            copy_of(step).wait()
            return carry

        lax.fori_loop(1, devices, start, 0)
        target[mine, :] = source[mine, :]
        lax.fori_loop(1, devices, finish, 0)

    def lane(values, index):
        return values[:, index * length : (index + 1) * length]

    def beside(values):
        lines = [
            jnp.concatenate([lane(values, p)[:length], lane(values, p)[length:]], axis=1)
            for p in range(own)
        ]
        return jnp.concatenate(lines, axis=0)

    def spread(c, plane, row):
        return pl.ds((c * own + plane) * rows + row, devices, stride=block)

    field = jnp.concatenate(
        [jnp.concatenate([dens[c, p] for c in range(2)], axis=0) for p in range(own)], axis=1
    )
    wave = times_table(beside(table_times(front_y, field)), right_front)
    for p in range(own):
        for row in range(rows):
            top = p * length + row * devices
            for c in range(2):
                away[spread(c, p, row), :] = lane(wave[top : top + devices], c)
    exchange(away, here, 0)
    field = jnp.concatenate(
        [
            jnp.concatenate(
                [here[spread(c, p, row), :] for c in range(2) for p in range(own)], axis=0
            )
            for row in range(rows)
        ],
        axis=1,
    )
    wave = table_times(front_x, field)
    weight = weights[...]
    wave = jnp.concatenate([wave[:length] * weight, wave[length:] * weight], axis=0)
    field = table_times(back_x, wave)
    for row in range(rows):
        for c in range(2):
            for p in range(own):
                top = (c * own + p) * devices
                back_away[spread(c, p, row), :] = lane(field[top : top + devices], row)
    exchange(back_away, back_here, 1)
    wave = jnp.concatenate(
        [
            jnp.concatenate(
                [back_here[spread(c, p, row), :] for c in range(2) for row in range(rows)], axis=0
            )
            for p in range(own)
        ],
        axis=1,
    )
    cell = times_table(beside(table_times(back_y, wave)), right_back)
    low = (2 * low_bit + high_bit) * own
    for p in range(own):
        for c in range(2):
            value = lane(cell[p * length : (p + 1) * length], c)
            out[c, low + p] = value + kernel[low + p] * dens[c, p]

    third = pair_copy(out.at[:, pl.ds(low, own)], out.at[:, pl.ds(low, own)], far, 2)
    third.start()
    third.wait()
    whole = pl.ds(low_bit * 2 * own, 2 * own)
    fourth = pair_copy(out.at[:, whole], out.at[:, whole], near, 3)
    fourth.start()
    fourth.wait()


def middle(grids, partial, kernel_xc):
    planes, length = partial.shape[1], partial.shape[2]
    devices = 4 * grids
    own, rows = planes // 4, length // devices
    turn = (2, 3, 0, 1)
    kept = np.arange(rows)[:, None] + rows * np.arange(devices)[None, :]
    kept = kept.reshape(-1)
    place = np.array([0, 2, 1, 3])
    numbers = (
        np.arange(own)[:, None, None]
        + own * place[None, :, None]
        + planes * np.arange(grids)[None, None, :]
    ).reshape(-1)
    mine = (lax.axis_index("band") * grids + lax.axis_index("grid")) * rows
    freqs = signed_freq(jnp.arange(length, dtype=jnp.int32), length)
    own_freqs = signed_freq(mine + jnp.arange(rows, dtype=jnp.int32), length)
    weights = coulomb(freqs, own_freqs, freqs, length).reshape(length, rows * length)
    operands = (
        partial,
        kernel_xc,
        weights,
        table_halves(dft_pair(length, -1.0, columns=kept).transpose(turn)),
        table_halves(dft_pair(length, -1.0)),
        table_halves(dft_pair(length, -1.0, rows=numbers).transpose(turn)),
        table_halves(dft_pair(length, 1.0, columns=numbers).transpose(turn)),
        table_halves(dft_pair(length, 1.0, rows=kept).transpose(turn)),
        table_halves(dft_pair(length, 1.0)),
    )
    parts = pltpu.VMEM((2 * own * length, length), jnp.float32)
    return pl.pallas_call(
        functools.partial(middle_kernel, grids),
        out_shape=jax.ShapeDtypeStruct(partial.shape, jnp.float32),
        in_specs=[pl.BlockSpec(memory_space=pltpu.VMEM)] * len(operands),
        out_specs=pl.BlockSpec(memory_space=pltpu.VMEM),
        scratch_shapes=[
            pltpu.VMEM((2, 2 * own, length, length), jnp.float32),
            pltpu.VMEM((2, 2 * own, length, length), jnp.float32),
            pltpu.VMEM((2, own, length, length), jnp.float32),
            pltpu.VMEM((2, own, length, length), jnp.float32),
            parts, parts, parts, parts,
            pltpu.SemaphoreType.DMA((4,)),
            pltpu.SemaphoreType.DMA((4,)),
            pltpu.SemaphoreType.DMA((2, devices)),
            pltpu.SemaphoreType.DMA((2, devices)),
        ],
        compiler_params=pltpu.CompilerParams(
            collective_id=2, has_side_effects=True, vmem_limit_bytes=40 * 2**20
        ),
    )(*operands)


def call(kernel, grids, rows, length, out_shape, by_source, collective_id, *operands):
    flat = (2, 2, length * rows, length)
    blocks = (2, grids, 2, rows * rows, length)
    return pl.pallas_call(
        functools.partial(kernel, grids),
        out_shape=jax.ShapeDtypeStruct(out_shape, jnp.float32),
        in_specs=[pl.BlockSpec(memory_space=pltpu.VMEM)] * len(operands),
        out_specs=pl.BlockSpec(memory_space=pltpu.VMEM),
        scratch_shapes=[
            pltpu.VMEM(flat if by_source else blocks, jnp.float32),
            pltpu.VMEM(blocks if by_source else flat, jnp.float32),
            pltpu.SemaphoreType.DMA((2, grids)),
            pltpu.SemaphoreType.DMA((2, grids)),
            pltpu.SemaphoreType.DMA((2,)),
        ],
        compiler_params=pltpu.CompilerParams(
            collective_id=collective_id, has_side_effects=True, vmem_limit_bytes=40 * 2**20
        ),
    )(*operands)


def ein(form, operand, table):
    return jnp.einsum(form, operand, table, precision=high)


def signed_freq(positions, length):
    return jnp.where(positions < (length + 1) // 2, positions, positions - length).astype(
        jnp.float32
    )


def coulomb(freq_first, freq_second, freq_third, length):
    squares = (
        freq_first[:, None, None] ** 2
        + freq_second[None, :, None] ** 2
        + freq_third[None, None, :] ** 2
    )
    edge_len = spacing * length
    return jnp.where(
        squares > 0.5, edge_len * edge_len / (math.pi * jnp.maximum(squares, 1.0)), 0.0
    )


def hartree(density, axes, device, devices, numbers):
    length = density.shape[-1]
    forward, backward = dft_pair(length, -1.0), dft_pair(length, 1.0)
    wave = ein("cxyz,cydk->dxkz", density, forward)
    wave = ein("dxkz,dzem->exkm", wave, forward)
    wave = lax.all_to_all(wave, axes, split_axis=2, concat_axis=1, tiled=True)
    rows = length // devices
    mine = device * rows + jnp.arange(rows, dtype=jnp.int32)
    freqs = signed_freq(jnp.arange(length, dtype=jnp.int32), length)
    weights = coulomb(freqs, signed_freq(mine, length), freqs, length)
    wave = ein("cxyz,cxdk->dkyz", wave, dft_pair(length, -1.0, rows=numbers)) * weights
    wave = ein("dkyz,dkex->exyz", wave, dft_pair(length, 1.0, columns=numbers))
    wave = lax.all_to_all(wave, axes, split_axis=1, concat_axis=2, tiled=True)
    cell = ein("dxkz,dzem->exkm", wave, backward)
    return ein("cxyz,cydk->dxkz", cell, backward)


def on_device(bands, grids, ground, response, kernel_xc):
    grid_len = ground.shape[2]
    planes = ground.shape[1]
    forward = dft_pair(grid_len, -1.0)
    backward = dft_pair(grid_len, 1.0)
    orbital = ground[0]

    flip = np.array([1.0, -1.0], np.float32)
    turn = (2, 3, 0, 1)
    left_y = np.stack([
        table_halves(backward.transpose(turn)),
        table_halves((backward * flip[:, None]).transpose(turn)),
    ])
    partial = call(
        arrive_kernel, grids, planes, grid_len, (2, planes, grid_len, grid_len), True, 0,
        response.reshape(2, 2, grid_len * planes, grid_len),
        orbital,
        table_halves(backward.transpose(turn)),
        table_halves(backward),
        left_y,
    )

    if bands == 4 and planes % 4 == 0 and grid_len % (4 * grids) == 0:
        pot = middle(grids, partial, kernel_xc)
    else:
        dens = lax.psum(partial, "band")
        pot = hartree(dens, "grid", lax.axis_index("grid"), grids, None)
        pot = pot + kernel_xc * dens

    left_y = np.stack([
        table_halves(forward.transpose(turn)),
        table_halves((forward * flip[:, None, None, None]).transpose(turn)),
    ])
    out = call(
        leave_kernel, grids, planes, grid_len, (2, 2, grid_len * planes, grid_len), False, 1,
        pot, orbital, left_y, table_halves(forward), table_halves(forward.transpose(turn)),
    )
    return out.reshape(1, 2, 2, grid_len, planes, grid_len)


def solution(mesh):
    bands, grids = mesh.shape["band"], mesh.shape["grid"]

    def body(ground, response, kernel_xc):
        return on_device(bands, grids, ground, response, kernel_xc)

    return jax.shard_map(
        body,
        mesh=mesh,
        in_specs=(
            P("band", "grid", None, None),
            P("band", None, None, None, "grid", None),
            P("grid", None, None),
        ),
        out_specs=P("band", None, None, None, "grid", None),
        check_vma=False,
    )
```

```python
import functools
import math

import jax
import jax.numpy as jnp
import ml_dtypes
import numpy as np
from jax import lax
from jax.experimental import pallas as pl
from jax.experimental.pallas import tpu as pltpu
from jax.sharding import PartitionSpec as P

high = lax.Precision.HIGH
spacing = 0.4527
width = 4


def dft_pair(length, direction, rows=None, columns=None):
    rows = np.arange(length) if rows is None else rows
    columns = np.arange(length) if columns is None else columns
    angles = (rows[:, None] * columns[None, :] % length) * (2.0 * math.pi / length)
    cosine = np.cos(angles) / math.sqrt(length)
    sine = direction * np.sin(angles) / math.sqrt(length)
    pairs = (np.stack((cosine, sine), axis=1), np.stack((-sine, cosine), axis=1))
    return np.stack(pairs, axis=0).astype(np.float32)


def halves(values):
    upper = values.astype(jnp.bfloat16)
    return upper, (values - upper.astype(jnp.float32)).astype(jnp.bfloat16)


def table_halves(table):
    values = table.reshape(2 * table.shape[1], -1)
    upper = values.astype(ml_dtypes.bfloat16)
    lower = (values - upper.astype(np.float32)).astype(ml_dtypes.bfloat16)
    return np.stack((upper, lower))


def dot(first, second):
    return jnp.dot(first, second, preferred_element_type=jnp.float32)


def times_table(values, table):
    upper, lower = halves(values)
    return dot(upper, table[0]) + (dot(upper, table[1]) + dot(lower, table[0]))


def table_times(table, values):
    upper, lower = halves(values)
    return dot(table[0], upper) + (dot(table[1], upper) + dot(table[0], lower))


def meet(group, devices):
    me = lax.axis_index(group)
    barrier = pltpu.get_barrier_semaphore()
    for step in range(1, devices):
        peer = lax.rem(me + step, devices)
        pl.semaphore_signal(
            barrier, inc=1, device_id={group: peer}, device_id_type=pl.DeviceIdType.MESH
        )
    pl.semaphore_wait(barrier, devices - 1)
    return me


def pieces(values, length):
    return [values[:, k * length : (k + 1) * length] for k in range(values.shape[1] // length)]


def transform_x(source, target, table, rows, length):
    def body(group, carry):
        column = []
        for k in range(width):
            picked = pl.ds(width * group + k, length, stride=rows)
            column.append(jnp.concatenate([source[c, picked, :] for c in range(2)], axis=0))
        wave = pieces(table_times(table, jnp.concatenate(column, axis=1)), length)
        for k in range(width):
            picked = pl.ds(width * group + k, length, stride=rows)
            for c in range(2):
                target[c, picked, :] = wave[k][c * length : (c + 1) * length]
        return carry

    lax.fori_loop(0, rows // width, body, 0)


def remote(source, target, sent, got, peer):
    copy = pltpu.make_async_remote_copy(
        src_ref=source, dst_ref=target, send_sem=sent, recv_sem=got,
        device_id={"grid": peer}, device_id_type=pl.DeviceIdType.MESH,
    )
    copy.start()
    return copy


def arrive(grids, resp, orbital, left_x, right_z, left_y, out, away, here, sent, got, own, ready):
    rows, length = orbital.shape[0], orbital.shape[1]
    block, part = rows * rows, rows * rows // 2
    me = lax.axis_index("grid")
    copies = {}
    for harmonic in range(2):
        transform_x(resp.at[harmonic], away.at[harmonic], left_x, rows, length)
        for half in range(2):
            kept = pl.ds(half * part, part)

            def taken(device):
                first = pl.multiple_of(device * block + half * part, part)
                return away.at[harmonic, :, pl.ds(first, part), :]

            mine = pltpu.make_async_copy(
                taken(me), here.at[harmonic, me, :, kept, :], own.at[harmonic, half]
            )
            mine.start()
            steps = []
            for step in range(1, grids):
                peer = lax.rem(me + step, grids)
                steps.append(
                    remote(
                        taken(peer), here.at[harmonic, me, :, kept, :],
                        sent.at[harmonic, half, step], got.at[harmonic, half, step], peer,
                    )
                )
            copies[harmonic, half] = (mine, steps)
    for harmonic in range(2):
        for half in range(2):
            mine, steps = copies[harmonic, half]
            mine.wait()
            for copy in steps:
                copy.wait_recv()

            def transform_zy(group, carry):
                lines = []
                for k in range(width):
                    plane = half * (rows // 2) + width * group + k
                    at = pl.ds(pl.multiple_of(plane * rows, rows), rows)
                    parts = [
                        jnp.concatenate([here[harmonic, s, c, at, :] for s in range(grids)], axis=0)
                        for c in range(2)
                    ]
                    lines.append(jnp.concatenate(parts, axis=1))
                wave = times_table(jnp.concatenate(lines, axis=0), right_z)
                planes = []
                for k in range(width):
                    line = wave[k * length : (k + 1) * length]
                    planes.append(jnp.concatenate(pieces(line, length), axis=0))
                cell = table_times(left_y[harmonic], jnp.concatenate(planes, axis=1))
                cell = pieces(cell, length)
                for k in range(width):
                    plane = half * (rows // 2) + width * group + k
                    for c in range(2):
                        value = cell[k][c * length : (c + 1) * length]
                        if harmonic == 0:
                            out[c, plane] = value
                        else:
                            out[c, plane] = (out[c, plane] + value) * orbital[plane]
                return carry

            lax.fori_loop(0, rows // 2 // width, transform_zy, 0)
            if harmonic == 1:
                ready(half)
    for mine, steps in copies.values():
        for copy in steps:
            copy.wait_send()


def leave(grids, pot, orbital, left_y, right_z, left_x, out, away, here, sent, got, own, need):
    rows, length = orbital.shape[0], orbital.shape[1]
    block, part = rows * rows, rows * rows // 2
    me = lax.axis_index("grid")
    copies = {}
    for half in range(2):
        need(half)
        kept = pl.ds(half * part, part)
        target = pl.ds(pl.multiple_of(me * block + half * part, part), part)
        for harmonic in range(2):

            def transform_yz(group, carry):
                planes = []
                for k in range(width):
                    plane = half * (rows // 2) + width * group + k
                    weight = orbital[plane]
                    planes.append(
                        jnp.concatenate([pot[c, plane] * weight for c in range(2)], axis=0)
                    )
                wave = table_times(left_y[harmonic], jnp.concatenate(planes, axis=1))
                lines = [
                    jnp.concatenate([piece[:length], piece[length:]], axis=1)
                    for piece in pieces(wave, length)
                ]
                wave = times_table(jnp.concatenate(lines, axis=0), right_z)
                for k in range(width):
                    plane = half * (rows // 2) + width * group + k
                    at = pl.ds(pl.multiple_of(plane * rows, rows), rows)
                    for s in range(grids):
                        first = k * length + s * rows
                        for c in range(2):
                            away[harmonic, s, c, at, :] = wave[
                                first : first + rows, c * length : (c + 1) * length
                            ]
                return carry

            lax.fori_loop(0, rows // 2 // width, transform_yz, 0)
            mine = pltpu.make_async_copy(
                away.at[harmonic, me, :, kept, :], here.at[harmonic, :, target, :],
                own.at[harmonic, half],
            )
            mine.start()
            steps = []
            for step in range(1, grids):
                peer = lax.rem(me + step, grids)
                steps.append(
                    remote(
                        away.at[harmonic, peer, :, kept, :], here.at[harmonic, :, target, :],
                        sent.at[harmonic, half, step], got.at[harmonic, half, step], peer,
                    )
                )
            copies[harmonic, half] = (mine, steps)
    for harmonic in range(2):
        for half in range(2):
            mine, steps = copies[harmonic, half]
            mine.wait()
            for copy in steps:
                copy.wait_recv()
        transform_x(here.at[harmonic], out.at[harmonic], left_x, rows, length)
    for mine, steps in copies.values():
        for copy in steps:
            copy.wait_send()


def nothing(half):
    del half


def arrive_kernel(grids, resp, orbital, tables, out, *scratch):
    meet("grid", grids)
    left_y = [tables.at[0], tables.at[1]]
    arrive(grids, resp, orbital, tables.at[0], tables.at[2], left_y, out, *scratch, nothing)


def leave_kernel(grids, pot, orbital, tables, out, *scratch):
    meet("grid", grids)
    left_y = [tables.at[3], tables.at[4]]
    leave(grids, pot, orbital, left_y, tables.at[5], tables.at[3], out, *scratch, nothing)


def basic_tables(length):
    tables = []
    turn = (2, 3, 0, 1)
    flip = np.array([1.0, -1.0], np.float32)
    backward, forward = dft_pair(length, 1.0), dft_pair(length, -1.0)
    tables.append(table_halves(backward.transpose(turn)))
    tables.append(table_halves((backward * flip[:, None]).transpose(turn)))
    tables.append(table_halves(backward))
    tables.append(table_halves(forward.transpose(turn)))
    tables.append(table_halves((forward * flip[:, None, None, None]).transpose(turn)))
    tables.append(table_halves(forward))
    return tables


def whole_kernel(
    grids, resp, orbital, kernel, weights, tables, result, part, got_half, half_sum, got_own, dens,
    away, here, back_away, back_here, out, in_away, in_here, out_away, out_here,
    pair_sent, pair_got, sent, got, in_sent, in_got, in_own, out_sent, out_got, out_own,
):
    devices = 4 * grids
    planes, length = part.shape[1], part.shape[2]
    own = planes // 4
    few = own // 2
    rows = length // devices
    block = 2 * own * rows
    band, grid = lax.axis_index("band"), lax.axis_index("grid")
    me = band * grids + grid

    def at(device):
        return {"band": device // grids, "grid": lax.rem(device, grids)}

    barrier = pltpu.get_barrier_semaphore()

    def greet(step, carry):
        pl.semaphore_signal(
            barrier, inc=1, device_id=at(lax.rem(me + step, devices)),
            device_id_type=pl.DeviceIdType.MESH,
        )
        return carry

    lax.fori_loop(1, devices, greet, 0)
    pl.semaphore_wait(barrier, devices - 1)

    low_bit, high_bit = lax.rem(band, 2), band // 2
    near = {"band": 2 * high_bit + (1 - low_bit), "grid": grid}
    far = {"band": 2 * (1 - high_bit) + low_bit, "grid": grid}

    def pair_copy(source, target, place, *index):
        return pltpu.make_async_remote_copy(
            src_ref=source, dst_ref=target, send_sem=pair_sent.at[index],
            recv_sem=pair_got.at[index], device_id=place, device_id_type=pl.DeviceIdType.MESH,
        )

    def add_bands(half):
        base = half * 2 * own
        kept = pl.ds(half * own, own)
        first = pair_copy(
            part.at[:, pl.ds(base + (1 - low_bit) * own, own)], got_half.at[:, kept], near, 0, half
        )
        first.start()
        first.wait()

        def add_half(plane, carry):
            for c in range(2):
                half_sum[c, half * own + plane] = (
                    part[c, base + low_bit * own + plane] + got_half[c, half * own + plane]
                )
            return carry

        lax.fori_loop(0, own, add_half, 0)
        second = pair_copy(
            half_sum.at[:, pl.ds(half * own + (1 - high_bit) * few, few)],
            got_own.at[:, pl.ds(half * few, few)], far, 1, half,
        )
        second.start()
        second.wait()
        for plane in range(few):
            for c in range(2):
                dens[c, half * few + plane] = (
                    half_sum[c, half * own + high_bit * few + plane]
                    + got_own[c, half * few + plane]
                )

    arrive(
        grids, resp, orbital, tables.at[0], tables.at[2], [tables.at[0], tables.at[1]], part,
        in_away, in_here, in_sent, in_got, in_own, add_bands,
    )

    def exchange(source, target, index):
        mine = pl.ds(pl.multiple_of(me * block, block), block)

        def copy_of(step):
            peer = lax.rem(me + step, devices)
            return pltpu.make_async_remote_copy(
                src_ref=source.at[pl.ds(pl.multiple_of(peer * block, block), block)],
                dst_ref=target.at[mine],
                send_sem=sent.at[index, step],
                recv_sem=got.at[index, step],
                device_id=at(peer),
                device_id_type=pl.DeviceIdType.MESH,
            )

        def start(step, carry):
            copy_of(step).start()
            return carry

        def finish(step, carry):
            copy_of(step).wait()
            return carry

        lax.fori_loop(1, devices, start, 0)
        target[mine, :] = source[mine, :]
        lax.fori_loop(1, devices, finish, 0)

    def lane(values, index):
        return values[:, index * length : (index + 1) * length]

    def beside(values):
        lines = [
            jnp.concatenate([lane(values, p)[:length], lane(values, p)[length:]], axis=1)
            for p in range(own)
        ]
        return jnp.concatenate(lines, axis=0)

    def spread(c, plane, row):
        return pl.ds((c * own + plane) * rows + row, devices, stride=block)

    field = jnp.concatenate(
        [jnp.concatenate([dens[c, p] for c in range(2)], axis=0) for p in range(own)], axis=1
    )
    wave = times_table(beside(table_times(tables.at[6], field)), tables.at[5])
    for p in range(own):
        for row in range(rows):
            top = p * length + row * devices
            for c in range(2):
                away[spread(c, p, row), :] = lane(wave[top : top + devices], c)
    exchange(away, here, 0)
    field = jnp.concatenate(
        [
            jnp.concatenate(
                [here[spread(c, p, row), :] for c in range(2) for p in range(own)], axis=0
            )
            for row in range(rows)
        ],
        axis=1,
    )
    wave = table_times(tables.at[7], field)
    weight = weights[...]
    wave = jnp.concatenate([wave[:length] * weight, wave[length:] * weight], axis=0)
    field = table_times(tables.at[8], wave)
    for row in range(rows):
        for c in range(2):
            for p in range(own):
                top = (c * own + p) * devices
                back_away[spread(c, p, row), :] = lane(field[top : top + devices], row)
    exchange(back_away, back_here, 1)
    wave = jnp.concatenate(
        [
            jnp.concatenate(
                [back_here[spread(c, p, row), :] for c in range(2) for row in range(rows)], axis=0
            )
            for p in range(own)
        ],
        axis=1,
    )
    cell = times_table(beside(table_times(tables.at[9], wave)), tables.at[2])
    third = []
    for half in range(2):
        low = half * 2 * own + low_bit * own + high_bit * few
        for q in range(few):
            p = half * few + q
            for c in range(2):
                value = lane(cell[p * length : (p + 1) * length], c)
                out[c, low + q] = value + kernel[low + q] * dens[c, p]
        mine = out.at[:, pl.ds(low, few)]
        third.append(pair_copy(mine, mine, far, 2, half))
        third[half].start()

    def gather(half):
        third[half].wait()
        mine = out.at[:, pl.ds(half * 2 * own + low_bit * own, own)]
        fourth = pair_copy(mine, mine, near, 3, half)
        fourth.start()
        fourth.wait()

    leave(
        grids, out, orbital, [tables.at[3], tables.at[4]], tables.at[5], tables.at[3], result,
        out_away, out_here, out_sent, out_got, out_own, gather,
    )


def whole(grids, response, orbital, kernel_xc):
    planes, length = orbital.shape[0], orbital.shape[1]
    devices = 4 * grids
    own, rows = planes // 4, length // devices
    few = own // 2
    turn = (2, 3, 0, 1)
    kept = np.arange(rows)[:, None] + rows * np.arange(devices)[None, :]
    kept = kept.reshape(-1)
    place = np.array([0, 2, 1, 3])
    plane = np.arange(own)
    numbers = (
        (plane // few * 2 * own + plane % few)[:, None, None]
        + few * place[None, :, None]
        + planes * np.arange(grids)[None, None, :]
    ).reshape(-1)
    mine = (lax.axis_index("band") * grids + lax.axis_index("grid")) * rows
    freqs = signed_freq(jnp.arange(length, dtype=jnp.int32), length)
    own_freqs = signed_freq(mine + jnp.arange(rows, dtype=jnp.int32), length)
    weights = coulomb(freqs, own_freqs, freqs, length).reshape(length, rows * length)
    tables = basic_tables(length) + [
        table_halves(dft_pair(length, -1.0, columns=kept).transpose(turn)),
        table_halves(dft_pair(length, -1.0, rows=numbers).transpose(turn)),
        table_halves(dft_pair(length, 1.0, columns=numbers).transpose(turn)),
        table_halves(dft_pair(length, 1.0, rows=kept).transpose(turn)),
    ]
    operands = (response, orbital, kernel_xc, weights, np.stack(tables))

    def space(*shape):
        return pltpu.VMEM(shape, jnp.float32)

    parts = space(2 * own * length, length)
    flat = space(2, 2, length * planes, length)
    blocks = space(2, grids, 2, planes * planes, length)
    wide = space(2, planes, length, length)
    meets = pltpu.SemaphoreType.DMA((2, 2, grids))
    return pl.pallas_call(
        functools.partial(whole_kernel, grids),
        out_shape=jax.ShapeDtypeStruct(response.shape, jnp.float32),
        in_specs=[pl.BlockSpec(memory_space=pltpu.VMEM)] * len(operands),
        out_specs=pl.BlockSpec(memory_space=pltpu.VMEM),
        scratch_shapes=[
            wide,
            space(2, 2 * own, length, length),
            space(2, 2 * own, length, length),
            space(2, own, length, length),
            space(2, own, length, length),
            parts, parts, parts, parts,
            wide,
            flat, blocks, blocks, flat,
            pltpu.SemaphoreType.DMA((4, 2)),
            pltpu.SemaphoreType.DMA((4, 2)),
            pltpu.SemaphoreType.DMA((2, devices)),
            pltpu.SemaphoreType.DMA((2, devices)),
            meets, meets, pltpu.SemaphoreType.DMA((2, 2)),
            meets, meets, pltpu.SemaphoreType.DMA((2, 2)),
        ],
        compiler_params=pltpu.CompilerParams(
            collective_id=2, has_side_effects=True, vmem_limit_bytes=56 * 2**20
        ),
    )(*operands)


def call(kernel, grids, rows, length, out_shape, by_source, collective_id, *operands):
    flat = (2, 2, length * rows, length)
    blocks = (2, grids, 2, rows * rows, length)
    return pl.pallas_call(
        functools.partial(kernel, grids),
        out_shape=jax.ShapeDtypeStruct(out_shape, jnp.float32),
        in_specs=[pl.BlockSpec(memory_space=pltpu.VMEM)] * len(operands),
        out_specs=pl.BlockSpec(memory_space=pltpu.VMEM),
        scratch_shapes=[
            pltpu.VMEM(flat if by_source else blocks, jnp.float32),
            pltpu.VMEM(blocks if by_source else flat, jnp.float32),
            pltpu.SemaphoreType.DMA((2, 2, grids)),
            pltpu.SemaphoreType.DMA((2, 2, grids)),
            pltpu.SemaphoreType.DMA((2, 2)),
        ],
        compiler_params=pltpu.CompilerParams(
            collective_id=collective_id, has_side_effects=True, vmem_limit_bytes=40 * 2**20
        ),
    )(*operands)


def ein(form, operand, table):
    return jnp.einsum(form, operand, table, precision=high)


def signed_freq(positions, length):
    return jnp.where(positions < (length + 1) // 2, positions, positions - length).astype(
        jnp.float32
    )


def coulomb(freq_first, freq_second, freq_third, length):
    squares = (
        freq_first[:, None, None] ** 2
        + freq_second[None, :, None] ** 2
        + freq_third[None, None, :] ** 2
    )
    edge_len = spacing * length
    return jnp.where(
        squares > 0.5, edge_len * edge_len / (math.pi * jnp.maximum(squares, 1.0)), 0.0
    )


def hartree(density, axes, device, devices, numbers):
    length = density.shape[-1]
    forward, backward = dft_pair(length, -1.0), dft_pair(length, 1.0)
    wave = ein("cxyz,cydk->dxkz", density, forward)
    wave = ein("dxkz,dzem->exkm", wave, forward)
    wave = lax.all_to_all(wave, axes, split_axis=2, concat_axis=1, tiled=True)
    rows = length // devices
    mine = device * rows + jnp.arange(rows, dtype=jnp.int32)
    freqs = signed_freq(jnp.arange(length, dtype=jnp.int32), length)
    weights = coulomb(freqs, signed_freq(mine, length), freqs, length)
    wave = ein("cxyz,cxdk->dkyz", wave, dft_pair(length, -1.0, rows=numbers)) * weights
    wave = ein("dkyz,dkex->exyz", wave, dft_pair(length, 1.0, columns=numbers))
    wave = lax.all_to_all(wave, axes, split_axis=1, concat_axis=2, tiled=True)
    cell = ein("dxkz,dzem->exkm", wave, backward)
    return ein("cxyz,cydk->dxkz", cell, backward)


def on_device(bands, grids, ground, response, kernel_xc):
    grid_len = ground.shape[2]
    planes = ground.shape[1]
    orbital = ground[0]
    flat = response.reshape(2, 2, grid_len * planes, grid_len)
    if bands == 4 and planes % 8 == 0 and grid_len % (4 * grids) == 0:
        out = whole(grids, flat, orbital, kernel_xc)
    else:
        tables = np.stack(basic_tables(grid_len))
        partial = call(
            arrive_kernel, grids, planes, grid_len, (2, planes, grid_len, grid_len), True, 0,
            flat, orbital, tables,
        )
        dens = lax.psum(partial, "band")
        pot = hartree(dens, "grid", lax.axis_index("grid"), grids, None) + kernel_xc * dens
        out = call(
            leave_kernel, grids, planes, grid_len, (2, 2, grid_len * planes, grid_len), False, 1,
            pot, orbital, tables,
        )
    return out.reshape(1, 2, 2, grid_len, planes, grid_len)


def solution(mesh):
    bands, grids = mesh.shape["band"], mesh.shape["grid"]

    def body(ground, response, kernel_xc):
        return on_device(bands, grids, ground, response, kernel_xc)

    return jax.shard_map(
        body,
        mesh=mesh,
        in_specs=(
            P("band", "grid", None, None),
            P("band", None, None, None, "grid", None),
            P("grid", None, None),
        ),
        out_specs=P("band", None, None, None, "grid", None),
        check_vma=False,
    )
```

```python
import functools
import math

import jax
import jax.numpy as jnp
import ml_dtypes
import numpy as np
from jax import lax
from jax.experimental import pallas as pl
from jax.experimental.pallas import tpu as pltpu
from jax.sharding import PartitionSpec as P

high = lax.Precision.HIGH
spacing = 0.4527
width = 4


def dft_pair(length, direction, rows=None, columns=None):
    rows = np.arange(length) if rows is None else rows
    columns = np.arange(length) if columns is None else columns
    angles = (rows[:, None] * columns[None, :] % length) * (2.0 * math.pi / length)
    cosine = np.cos(angles) / math.sqrt(length)
    sine = direction * np.sin(angles) / math.sqrt(length)
    pairs = (np.stack((cosine, sine), axis=1), np.stack((-sine, cosine), axis=1))
    return np.stack(pairs, axis=0).astype(np.float32)


def halves(values):
    upper = values.astype(jnp.bfloat16)
    return upper, (values - upper.astype(jnp.float32)).astype(jnp.bfloat16)


def table_halves(table):
    values = table.reshape(2 * table.shape[1], -1)
    upper = values.astype(ml_dtypes.bfloat16)
    lower = (values - upper.astype(np.float32)).astype(ml_dtypes.bfloat16)
    return np.stack((upper, lower))


def dot(first, second):
    return jnp.dot(first, second, preferred_element_type=jnp.float32)


def times_table(values, table):
    upper, lower = halves(values)
    return dot(upper, table[0]) + (dot(upper, table[1]) + dot(lower, table[0]))


def table_times(table, values):
    upper, lower = halves(values)
    return dot(table[0], upper) + (dot(table[1], upper) + dot(table[0], lower))


def meet(group, devices):
    me = lax.axis_index(group)
    barrier = pltpu.get_barrier_semaphore()
    for step in range(1, devices):
        peer = lax.rem(me + step, devices)
        pl.semaphore_signal(
            barrier, inc=1, device_id={group: peer}, device_id_type=pl.DeviceIdType.MESH
        )
    pl.semaphore_wait(barrier, devices - 1)
    return me


def pieces(values, length):
    return [values[:, k * length : (k + 1) * length] for k in range(values.shape[1] // length)]


def transform_x(source, target, table, rows, length):
    def body(group, carry):
        column = []
        for k in range(width):
            picked = pl.ds(width * group + k, length, stride=rows)
            column.append(jnp.concatenate([source[c, picked, :] for c in range(2)], axis=0))
        wave = pieces(table_times(table, jnp.concatenate(column, axis=1)), length)
        for k in range(width):
            picked = pl.ds(width * group + k, length, stride=rows)
            for c in range(2):
                target[c, picked, :] = wave[k][c * length : (c + 1) * length]
        return carry

    lax.fori_loop(0, rows // width, body, 0)


def far_first(devices):
    return sorted(range(1, devices), key=lambda step: abs(2 * step - devices))


def remote(source, target, sent, got, peer):
    copy = pltpu.make_async_remote_copy(
        src_ref=source, dst_ref=target, send_sem=sent, recv_sem=got,
        device_id={"grid": peer}, device_id_type=pl.DeviceIdType.MESH,
    )
    copy.start()
    return copy


def arrive(grids, resp, orbital, left_x, right_z, left_y, out, away, here, sent, got, own, ready, before):
    rows, length = orbital.shape[0], orbital.shape[1]
    block, part = rows * rows, rows * rows // 2
    me = lax.axis_index("grid")
    copies = {}
    for harmonic in range(2):
        before(harmonic)
        transform_x(resp.at[harmonic], away.at[harmonic], left_x, rows, length)
        for half in range(2):
            kept = pl.ds(half * part, part)

            def taken(device):
                first = pl.multiple_of(device * block + half * part, part)
                return away.at[harmonic, :, pl.ds(first, part), :]

            mine = pltpu.make_async_copy(
                taken(me), here.at[harmonic, me, :, kept, :], own.at[harmonic, half]
            )
            mine.start()
            steps = []
            for step in far_first(grids):
                peer = lax.rem(me + step, grids)
                steps.append(
                    remote(
                        taken(peer), here.at[harmonic, me, :, kept, :],
                        sent.at[harmonic, half, step], got.at[harmonic, half, step], peer,
                    )
                )
            copies[harmonic, half] = (mine, steps)
    before(2)
    for harmonic in range(2):
        for half in range(2):
            mine, steps = copies[harmonic, half]
            mine.wait()
            for copy in steps:
                copy.wait_recv()

            def transform_zy(group, carry):
                lines = []
                for k in range(width):
                    plane = half * (rows // 2) + width * group + k
                    at = pl.ds(pl.multiple_of(plane * rows, rows), rows)
                    parts = [
                        jnp.concatenate([here[harmonic, s, c, at, :] for s in range(grids)], axis=0)
                        for c in range(2)
                    ]
                    lines.append(jnp.concatenate(parts, axis=1))
                wave = times_table(jnp.concatenate(lines, axis=0), right_z)
                planes = []
                for k in range(width):
                    line = wave[k * length : (k + 1) * length]
                    planes.append(jnp.concatenate(pieces(line, length), axis=0))
                cell = table_times(left_y[harmonic], jnp.concatenate(planes, axis=1))
                cell = pieces(cell, length)
                for k in range(width):
                    plane = half * (rows // 2) + width * group + k
                    for c in range(2):
                        value = cell[k][c * length : (c + 1) * length]
                        if harmonic == 0:
                            out[c, plane] = value
                        else:
                            out[c, plane] = (out[c, plane] + value) * orbital[plane]
                return carry

            lax.fori_loop(0, rows // 2 // width, transform_zy, 0)
            if harmonic == 1:
                ready(half)
    for mine, steps in copies.values():
        for copy in steps:
            copy.wait_send()


def leave(grids, pot, orbital, left_y, right_z, left_x, out, away, here, sent, got, own, need, done):
    rows, length = orbital.shape[0], orbital.shape[1]
    block, part = rows * rows, rows * rows // 2
    me = lax.axis_index("grid")
    copies = {}
    for half in range(2):
        need(half)
        kept = pl.ds(half * part, part)
        target = pl.ds(pl.multiple_of(me * block + half * part, part), part)
        for harmonic in range(2):

            def transform_yz(group, carry):
                planes = []
                for k in range(width):
                    plane = half * (rows // 2) + width * group + k
                    weight = orbital[plane]
                    planes.append(
                        jnp.concatenate([pot[c, plane] * weight for c in range(2)], axis=0)
                    )
                wave = table_times(left_y[harmonic], jnp.concatenate(planes, axis=1))
                lines = [
                    jnp.concatenate([piece[:length], piece[length:]], axis=1)
                    for piece in pieces(wave, length)
                ]
                wave = times_table(jnp.concatenate(lines, axis=0), right_z)
                for k in range(width):
                    plane = half * (rows // 2) + width * group + k
                    at = pl.ds(pl.multiple_of(plane * rows, rows), rows)
                    for s in range(grids):
                        first = k * length + s * rows
                        for c in range(2):
                            away[harmonic, s, c, at, :] = wave[
                                first : first + rows, c * length : (c + 1) * length
                            ]
                return carry

            lax.fori_loop(0, rows // 2 // width, transform_yz, 0)
            mine = pltpu.make_async_copy(
                away.at[harmonic, me, :, kept, :], here.at[harmonic, :, target, :],
                own.at[harmonic, half],
            )
            mine.start()
            steps = []
            for step in far_first(grids):
                peer = lax.rem(me + step, grids)
                steps.append(
                    remote(
                        away.at[harmonic, peer, :, kept, :], here.at[harmonic, :, target, :],
                        sent.at[harmonic, half, step], got.at[harmonic, half, step], peer,
                    )
                )
            copies[harmonic, half] = (mine, steps)
    for harmonic in range(2):
        for half in range(2):
            mine, steps = copies[harmonic, half]
            mine.wait()
            for copy in steps:
                copy.wait_recv()
        transform_x(here.at[harmonic], out.at[harmonic], left_x, rows, length)
        done(harmonic)
    for mine, steps in copies.values():
        for copy in steps:
            copy.wait_send()


def nothing(half):
    del half


def arrive_kernel(grids, resp, orbital, tables, out, *scratch):
    meet("grid", grids)
    left_y = [tables.at[0], tables.at[1]]
    arrive(grids, resp, orbital, tables.at[0], tables.at[2], left_y, out, *scratch, nothing, nothing)


def leave_kernel(grids, pot, orbital, tables, out, *scratch):
    meet("grid", grids)
    left_y = [tables.at[3], tables.at[4]]
    leave(grids, pot, orbital, left_y, tables.at[5], tables.at[3], out, *scratch, nothing, nothing)


def basic_tables(length):
    tables = []
    turn = (2, 3, 0, 1)
    flip = np.array([1.0, -1.0], np.float32)
    backward, forward = dft_pair(length, 1.0), dft_pair(length, -1.0)
    tables.append(table_halves(backward.transpose(turn)))
    tables.append(table_halves((backward * flip[:, None]).transpose(turn)))
    tables.append(table_halves(backward))
    tables.append(table_halves(forward.transpose(turn)))
    tables.append(table_halves((forward * flip[:, None, None, None]).transpose(turn)))
    tables.append(table_halves(forward))
    return tables


def whole_kernel(
    grids, resp_far, orbital_far, kernel_far, tables_far, weights, result_far, resp, orbital,
    kernel, tables, result, moved, part, got_half, half_sum, got_own, dens,
    away, here, back_away, back_here, out, in_away, in_here, out_away, out_here,
    pair_sent, pair_got, sent, got, in_sent, in_got, in_own, out_sent, out_got, out_own,
):
    devices = 4 * grids
    planes, length = part.shape[1], part.shape[2]
    own = planes // 4
    few = own // 2
    rows = length // devices
    block = 2 * own * rows
    band, grid = lax.axis_index("band"), lax.axis_index("grid")
    me = band * grids + grid

    def load(source, target, index):
        copy = pltpu.make_async_copy(source, target, moved.at[index])
        copy.start()
        return copy

    count = tables.shape[0]
    loads = [
        load(tables_far.at[pl.ds(0, 1)], tables.at[pl.ds(0, 1)], 0),
        load(resp_far.at[0], resp.at[0], 1),
        load(resp_far.at[1], resp.at[1], 2),
        load(tables_far.at[pl.ds(1, count - 1)], tables.at[pl.ds(1, count - 1)], 3),
        load(orbital_far, orbital, 4),
        load(kernel_far, kernel, 5),
    ]

    def before(stage):
        for copy in (loads[:2], loads[2:3], loads[3:])[stage]:
            copy.wait()

    stores = []

    def done(harmonic):
        stores.append(load(result.at[harmonic], result_far.at[harmonic], 6 + harmonic))

    def at(device):
        return {"band": device // grids, "grid": lax.rem(device, grids)}

    barrier = pltpu.get_barrier_semaphore()

    def greet(step, carry):
        pl.semaphore_signal(
            barrier, inc=1, device_id=at(lax.rem(me + step, devices)),
            device_id_type=pl.DeviceIdType.MESH,
        )
        return carry

    lax.fori_loop(1, devices, greet, 0)
    pl.semaphore_wait(barrier, devices - 1)

    low_bit, high_bit = lax.rem(band, 2), band // 2
    near = {"band": 2 * high_bit + (1 - low_bit), "grid": grid}
    far = {"band": 2 * (1 - high_bit) + low_bit, "grid": grid}

    def pair_copy(source, target, place, *index):
        return pltpu.make_async_remote_copy(
            src_ref=source, dst_ref=target, send_sem=pair_sent.at[index],
            recv_sem=pair_got.at[index], device_id=place, device_id_type=pl.DeviceIdType.MESH,
        )

    def add_bands(half):
        base = half * 2 * own
        kept = pl.ds(half * own, own)
        first = pair_copy(
            part.at[:, pl.ds(base + (1 - low_bit) * own, own)], got_half.at[:, kept], near, 0, half
        )
        first.start()
        first.wait()

        def add_half(plane, carry):
            for c in range(2):
                half_sum[c, half * own + plane] = (
                    part[c, base + low_bit * own + plane] + got_half[c, half * own + plane]
                )
            return carry

        lax.fori_loop(0, own, add_half, 0)
        second = pair_copy(
            half_sum.at[:, pl.ds(half * own + (1 - high_bit) * few, few)],
            got_own.at[:, pl.ds(half * few, few)], far, 1, half,
        )
        second.start()
        second.wait()
        for plane in range(few):
            for c in range(2):
                dens[c, half * few + plane] = (
                    half_sum[c, half * own + high_bit * few + plane]
                    + got_own[c, half * few + plane]
                )

    arrive(
        grids, resp, orbital, tables.at[0], tables.at[2], [tables.at[0], tables.at[1]], part,
        in_away, in_here, in_sent, in_got, in_own, add_bands, before,
    )

    def exchange(source, target, index):
        mine = pl.ds(pl.multiple_of(me * block, block), block)

        def copy_of(step):
            peer = lax.rem(me + step, devices)
            return pltpu.make_async_remote_copy(
                src_ref=source.at[pl.ds(pl.multiple_of(peer * block, block), block)],
                dst_ref=target.at[mine],
                send_sem=sent.at[index, step],
                recv_sem=got.at[index, step],
                device_id=at(peer),
                device_id_type=pl.DeviceIdType.MESH,
            )

        def start(step, carry):
            copy_of(step).start()
            return carry

        def finish(step, carry):
            copy_of(step).wait()
            return carry

        lax.fori_loop(1, devices, start, 0)
        target[mine, :] = source[mine, :]
        lax.fori_loop(1, devices, finish, 0)

    def lane(values, index):
        return values[:, index * length : (index + 1) * length]

    def beside(values):
        lines = [
            jnp.concatenate([lane(values, p)[:length], lane(values, p)[length:]], axis=1)
            for p in range(own)
        ]
        return jnp.concatenate(lines, axis=0)

    def spread(c, plane, row):
        return pl.ds((c * own + plane) * rows + row, devices, stride=block)

    field = jnp.concatenate(
        [jnp.concatenate([dens[c, p] for c in range(2)], axis=0) for p in range(own)], axis=1
    )
    wave = times_table(beside(table_times(tables.at[6], field)), tables.at[5])
    for p in range(own):
        for row in range(rows):
            top = p * length + row * devices
            for c in range(2):
                away[spread(c, p, row), :] = lane(wave[top : top + devices], c)
    exchange(away, here, 0)
    field = jnp.concatenate(
        [
            jnp.concatenate(
                [here[spread(c, p, row), :] for c in range(2) for p in range(own)], axis=0
            )
            for row in range(rows)
        ],
        axis=1,
    )
    wave = table_times(tables.at[7], field)
    weight = weights[...]
    wave = jnp.concatenate([wave[:length] * weight, wave[length:] * weight], axis=0)
    field = table_times(tables.at[8], wave)
    for row in range(rows):
        for c in range(2):
            for p in range(own):
                top = (c * own + p) * devices
                back_away[spread(c, p, row), :] = lane(field[top : top + devices], row)
    exchange(back_away, back_here, 1)
    wave = jnp.concatenate(
        [
            jnp.concatenate(
                [back_here[spread(c, p, row), :] for c in range(2) for row in range(rows)], axis=0
            )
            for p in range(own)
        ],
        axis=1,
    )
    cell = times_table(beside(table_times(tables.at[9], wave)), tables.at[2])
    third = []
    for half in range(2):
        low = half * 2 * own + low_bit * own + high_bit * few
        for q in range(few):
            p = half * few + q
            for c in range(2):
                value = lane(cell[p * length : (p + 1) * length], c)
                out[c, low + q] = value + kernel[low + q] * dens[c, p]
        mine = out.at[:, pl.ds(low, few)]
        third.append(pair_copy(mine, mine, far, 2, half))
        third[half].start()

    def gather(half):
        third[half].wait()
        mine = out.at[:, pl.ds(half * 2 * own + low_bit * own, own)]
        fourth = pair_copy(mine, mine, near, 3, half)
        fourth.start()
        fourth.wait()

    leave(
        grids, out, orbital, [tables.at[3], tables.at[4]], tables.at[5], tables.at[3], result,
        out_away, out_here, out_sent, out_got, out_own, gather, done,
    )
    for copy in stores:
        copy.wait()


def whole(grids, response, orbital, kernel_xc):
    planes, length = orbital.shape[0], orbital.shape[1]
    devices = 4 * grids
    own, rows = planes // 4, length // devices
    few = own // 2
    turn = (2, 3, 0, 1)
    kept = np.arange(rows)[:, None] + rows * np.arange(devices)[None, :]
    kept = kept.reshape(-1)
    place = np.array([0, 2, 1, 3])
    plane = np.arange(own)
    numbers = (
        (plane // few * 2 * own + plane % few)[:, None, None]
        + few * place[None, :, None]
        + planes * np.arange(grids)[None, None, :]
    ).reshape(-1)
    mine = (lax.axis_index("band") * grids + lax.axis_index("grid")) * rows
    freqs = signed_freq(jnp.arange(length, dtype=jnp.int32), length)
    own_freqs = signed_freq(mine + jnp.arange(rows, dtype=jnp.int32), length)
    weights = coulomb(freqs, own_freqs, freqs, length).reshape(length, rows * length)
    tables = basic_tables(length) + [
        table_halves(dft_pair(length, -1.0, columns=kept).transpose(turn)),
        table_halves(dft_pair(length, -1.0, rows=numbers).transpose(turn)),
        table_halves(dft_pair(length, 1.0, columns=numbers).transpose(turn)),
        table_halves(dft_pair(length, 1.0, rows=kept).transpose(turn)),
    ]
    operands = (response, orbital, kernel_xc, np.stack(tables), weights)

    def space(*shape):
        return pltpu.VMEM(shape, jnp.float32)

    parts = space(2 * own * length, length)
    flat = space(2, 2, length * planes, length)
    blocks = space(2, grids, 2, planes * planes, length)
    wide = space(2, planes, length, length)
    meets = pltpu.SemaphoreType.DMA((2, 2, grids))
    return pl.pallas_call(
        functools.partial(whole_kernel, grids),
        out_shape=jax.ShapeDtypeStruct(response.shape, jnp.float32),
        in_specs=[pl.BlockSpec(memory_space=pl.ANY)] * 4
        + [pl.BlockSpec(memory_space=pltpu.VMEM)],
        out_specs=pl.BlockSpec(memory_space=pl.ANY),
        scratch_shapes=[
            flat,
            space(planes, length, length),
            space(planes, length, length),
            pltpu.VMEM((len(tables), 2, 2 * length, 2 * length), jnp.bfloat16),
            flat,
            pltpu.SemaphoreType.DMA((8,)),
            wide,
            space(2, 2 * own, length, length),
            space(2, 2 * own, length, length),
            space(2, own, length, length),
            space(2, own, length, length),
            parts, parts, parts, parts,
            wide,
            flat, blocks, blocks, flat,
            pltpu.SemaphoreType.DMA((4, 2)),
            pltpu.SemaphoreType.DMA((4, 2)),
            pltpu.SemaphoreType.DMA((2, devices)),
            pltpu.SemaphoreType.DMA((2, devices)),
            meets, meets, pltpu.SemaphoreType.DMA((2, 2)),
            meets, meets, pltpu.SemaphoreType.DMA((2, 2)),
        ],
        compiler_params=pltpu.CompilerParams(
            collective_id=2, has_side_effects=True, vmem_limit_bytes=56 * 2**20
        ),
    )(*operands)


def call(kernel, grids, rows, length, out_shape, by_source, collective_id, *operands):
    flat = (2, 2, length * rows, length)
    blocks = (2, grids, 2, rows * rows, length)
    return pl.pallas_call(
        functools.partial(kernel, grids),
        out_shape=jax.ShapeDtypeStruct(out_shape, jnp.float32),
        in_specs=[pl.BlockSpec(memory_space=pltpu.VMEM)] * len(operands),
        out_specs=pl.BlockSpec(memory_space=pltpu.VMEM),
        scratch_shapes=[
            pltpu.VMEM(flat if by_source else blocks, jnp.float32),
            pltpu.VMEM(blocks if by_source else flat, jnp.float32),
            pltpu.SemaphoreType.DMA((2, 2, grids)),
            pltpu.SemaphoreType.DMA((2, 2, grids)),
            pltpu.SemaphoreType.DMA((2, 2)),
        ],
        compiler_params=pltpu.CompilerParams(
            collective_id=collective_id, has_side_effects=True, vmem_limit_bytes=40 * 2**20
        ),
    )(*operands)


def ein(form, operand, table):
    return jnp.einsum(form, operand, table, precision=high)


def signed_freq(positions, length):
    return jnp.where(positions < (length + 1) // 2, positions, positions - length).astype(
        jnp.float32
    )


def coulomb(freq_first, freq_second, freq_third, length):
    squares = (
        freq_first[:, None, None] ** 2
        + freq_second[None, :, None] ** 2
        + freq_third[None, None, :] ** 2
    )
    edge_len = spacing * length
    return jnp.where(
        squares > 0.5, edge_len * edge_len / (math.pi * jnp.maximum(squares, 1.0)), 0.0
    )


def hartree(density, axes, device, devices, numbers):
    length = density.shape[-1]
    forward, backward = dft_pair(length, -1.0), dft_pair(length, 1.0)
    wave = ein("cxyz,cydk->dxkz", density, forward)
    wave = ein("dxkz,dzem->exkm", wave, forward)
    wave = lax.all_to_all(wave, axes, split_axis=2, concat_axis=1, tiled=True)
    rows = length // devices
    mine = device * rows + jnp.arange(rows, dtype=jnp.int32)
    freqs = signed_freq(jnp.arange(length, dtype=jnp.int32), length)
    weights = coulomb(freqs, signed_freq(mine, length), freqs, length)
    wave = ein("cxyz,cxdk->dkyz", wave, dft_pair(length, -1.0, rows=numbers)) * weights
    wave = ein("dkyz,dkex->exyz", wave, dft_pair(length, 1.0, columns=numbers))
    wave = lax.all_to_all(wave, axes, split_axis=1, concat_axis=2, tiled=True)
    cell = ein("dxkz,dzem->exkm", wave, backward)
    return ein("cxyz,cydk->dxkz", cell, backward)


def on_device(bands, grids, ground, response, kernel_xc):
    grid_len = ground.shape[2]
    planes = ground.shape[1]
    orbital = ground[0]
    flat = response.reshape(2, 2, grid_len * planes, grid_len)
    if bands == 4 and planes % 8 == 0 and grid_len % (4 * grids) == 0:
        out = whole(grids, flat, orbital, kernel_xc)
    else:
        tables = np.stack(basic_tables(grid_len))
        partial = call(
            arrive_kernel, grids, planes, grid_len, (2, planes, grid_len, grid_len), True, 0,
            flat, orbital, tables,
        )
        dens = lax.psum(partial, "band")
        pot = hartree(dens, "grid", lax.axis_index("grid"), grids, None) + kernel_xc * dens
        out = call(
            leave_kernel, grids, planes, grid_len, (2, 2, grid_len * planes, grid_len), False, 1,
            pot, orbital, tables,
        )
    return out.reshape(1, 2, 2, grid_len, planes, grid_len)


def solution(mesh):
    bands, grids = mesh.shape["band"], mesh.shape["grid"]

    def body(ground, response, kernel_xc):
        return on_device(bands, grids, ground, response, kernel_xc)

    return jax.shard_map(
        body,
        mesh=mesh,
        in_specs=(
            P("band", "grid", None, None),
            P("band", None, None, None, "grid", None),
            P("grid", None, None),
        ),
        out_specs=P("band", None, None, None, "grid", None),
        check_vma=False,
    )
```

```python
import functools
import math

import jax
import jax.numpy as jnp
import ml_dtypes
import numpy as np
from jax import lax
from jax.experimental import pallas as pl
from jax.experimental.pallas import tpu as pltpu
from jax.sharding import PartitionSpec as P

high = lax.Precision.HIGH
spacing = 0.4527
width = 4


def dft_pair(length, direction, rows=None, columns=None):
    rows = np.arange(length) if rows is None else rows
    columns = np.arange(length) if columns is None else columns
    angles = (rows[:, None] * columns[None, :] % length) * (2.0 * math.pi / length)
    cosine = np.cos(angles) / math.sqrt(length)
    sine = direction * np.sin(angles) / math.sqrt(length)
    pairs = (np.stack((cosine, sine), axis=1), np.stack((-sine, cosine), axis=1))
    return np.stack(pairs, axis=0).astype(np.float32)


def halves(values):
    upper = values.astype(jnp.bfloat16)
    return upper, (values - upper.astype(jnp.float32)).astype(jnp.bfloat16)


def table_halves(table):
    values = table.reshape(2 * table.shape[1], -1)
    upper = values.astype(ml_dtypes.bfloat16)
    lower = (values - upper.astype(np.float32)).astype(ml_dtypes.bfloat16)
    return np.stack((upper, lower))


def dot(first, second):
    return jnp.dot(first, second, preferred_element_type=jnp.float32)


def times_table(values, table):
    upper, lower = halves(values)
    count = values.shape[0]
    both = dot(jnp.concatenate((upper, lower), axis=0), table[0])
    return both[:count] + (dot(upper, table[1]) + both[count:])


def table_times(table, values):
    upper, lower = halves(values)
    count = table.shape[1]
    both = dot(jnp.concatenate((table[0], table[1]), axis=0), upper)
    return both[:count] + (both[count:] + dot(table[0], lower))


def meet(group, devices):
    me = lax.axis_index(group)
    barrier = pltpu.get_barrier_semaphore()
    for step in range(1, devices):
        peer = lax.rem(me + step, devices)
        pl.semaphore_signal(
            barrier, inc=1, device_id={group: peer}, device_id_type=pl.DeviceIdType.MESH
        )
    pl.semaphore_wait(barrier, devices - 1)
    return me


def pieces(values, length):
    return [values[:, k * length : (k + 1) * length] for k in range(values.shape[1] // length)]


def transform_x(source, target, table, rows, length):
    def body(group, carry):
        column = []
        for k in range(width):
            picked = pl.ds(width * group + k, length, stride=rows)
            column.append(jnp.concatenate([source[c, picked, :] for c in range(2)], axis=0))
        wave = pieces(table_times(table, jnp.concatenate(column, axis=1)), length)
        for k in range(width):
            picked = pl.ds(width * group + k, length, stride=rows)
            for c in range(2):
                target[c, picked, :] = wave[k][c * length : (c + 1) * length]
        return carry

    lax.fori_loop(0, rows // width, body, 0)


def far_first(devices):
    return sorted(range(1, devices), key=lambda step: abs(2 * step - devices))


def remote(source, target, sent, got, peer):
    copy = pltpu.make_async_remote_copy(
        src_ref=source, dst_ref=target, send_sem=sent, recv_sem=got,
        device_id={"grid": peer}, device_id_type=pl.DeviceIdType.MESH,
    )
    copy.start()
    return copy


def arrive(grids, resp, orbital, left_x, right_z, left_y, out, away, here, sent, got, own, ready, before):
    rows, length = orbital.shape[0], orbital.shape[1]
    block, part = rows * rows, rows * rows // 2
    me = lax.axis_index("grid")
    copies = {}
    for harmonic in range(2):
        before(harmonic)
        transform_x(resp.at[harmonic], away.at[harmonic], left_x, rows, length)
        for half in range(2):
            kept = pl.ds(half * part, part)

            def taken(device):
                first = pl.multiple_of(device * block + half * part, part)
                return away.at[harmonic, :, pl.ds(first, part), :]

            mine = pltpu.make_async_copy(
                taken(me), here.at[harmonic, me, :, kept, :], own.at[harmonic, half]
            )
            mine.start()
            steps = []
            for step in far_first(grids):
                peer = lax.rem(me + step, grids)
                steps.append(
                    remote(
                        taken(peer), here.at[harmonic, me, :, kept, :],
                        sent.at[harmonic, half, step], got.at[harmonic, half, step], peer,
                    )
                )
            copies[harmonic, half] = (mine, steps)
    before(2)
    for harmonic in range(2):
        for half in range(2):
            mine, steps = copies[harmonic, half]
            mine.wait()
            for copy in steps:
                copy.wait_recv()

            def transform_zy(group, carry):
                lines = []
                for k in range(width):
                    plane = half * (rows // 2) + width * group + k
                    at = pl.ds(pl.multiple_of(plane * rows, rows), rows)
                    parts = [
                        jnp.concatenate([here[harmonic, s, c, at, :] for s in range(grids)], axis=0)
                        for c in range(2)
                    ]
                    lines.append(jnp.concatenate(parts, axis=1))
                wave = times_table(jnp.concatenate(lines, axis=0), right_z)
                planes = []
                for k in range(width):
                    line = wave[k * length : (k + 1) * length]
                    planes.append(jnp.concatenate(pieces(line, length), axis=0))
                cell = table_times(left_y[harmonic], jnp.concatenate(planes, axis=1))
                cell = pieces(cell, length)
                for k in range(width):
                    plane = half * (rows // 2) + width * group + k
                    for c in range(2):
                        value = cell[k][c * length : (c + 1) * length]
                        if harmonic == 0:
                            out[c, plane] = value
                        else:
                            out[c, plane] = (out[c, plane] + value) * orbital[plane]
                return carry

            lax.fori_loop(0, rows // 2 // width, transform_zy, 0)
            if harmonic == 1:
                ready(half)
    for mine, steps in copies.values():
        for copy in steps:
            copy.wait_send()


def leave(grids, pot, orbital, left_y, right_z, left_x, out, away, here, sent, got, own, need, done):
    rows, length = orbital.shape[0], orbital.shape[1]
    block, part = rows * rows, rows * rows // 2
    me = lax.axis_index("grid")
    copies = {}
    for half in range(2):
        need(half)
        kept = pl.ds(half * part, part)
        target = pl.ds(pl.multiple_of(me * block + half * part, part), part)
        for harmonic in range(2):

            def transform_yz(group, carry):
                planes = []
                for k in range(width):
                    plane = half * (rows // 2) + width * group + k
                    weight = orbital[plane]
                    planes.append(
                        jnp.concatenate([pot[c, plane] * weight for c in range(2)], axis=0)
                    )
                wave = table_times(left_y[harmonic], jnp.concatenate(planes, axis=1))
                lines = [
                    jnp.concatenate([piece[:length], piece[length:]], axis=1)
                    for piece in pieces(wave, length)
                ]
                wave = times_table(jnp.concatenate(lines, axis=0), right_z)
                for k in range(width):
                    plane = half * (rows // 2) + width * group + k
                    at = pl.ds(pl.multiple_of(plane * rows, rows), rows)
                    for s in range(grids):
                        first = k * length + s * rows
                        for c in range(2):
                            away[harmonic, s, c, at, :] = wave[
                                first : first + rows, c * length : (c + 1) * length
                            ]
                return carry

            lax.fori_loop(0, rows // 2 // width, transform_yz, 0)
            mine = pltpu.make_async_copy(
                away.at[harmonic, me, :, kept, :], here.at[harmonic, :, target, :],
                own.at[harmonic, half],
            )
            mine.start()
            steps = []
            for step in far_first(grids):
                peer = lax.rem(me + step, grids)
                steps.append(
                    remote(
                        away.at[harmonic, peer, :, kept, :], here.at[harmonic, :, target, :],
                        sent.at[harmonic, half, step], got.at[harmonic, half, step], peer,
                    )
                )
            copies[harmonic, half] = (mine, steps)
    for harmonic in range(2):
        for half in range(2):
            mine, steps = copies[harmonic, half]
            mine.wait()
            for copy in steps:
                copy.wait_recv()
        transform_x(here.at[harmonic], out.at[harmonic], left_x, rows, length)
        done(harmonic)
    for mine, steps in copies.values():
        for copy in steps:
            copy.wait_send()


def nothing(half):
    del half


def arrive_kernel(grids, resp, orbital, tables, out, *scratch):
    meet("grid", grids)
    left_y = [tables.at[0], tables.at[1]]
    arrive(grids, resp, orbital, tables.at[0], tables.at[2], left_y, out, *scratch, nothing, nothing)


def leave_kernel(grids, pot, orbital, tables, out, *scratch):
    meet("grid", grids)
    left_y = [tables.at[3], tables.at[4]]
    leave(grids, pot, orbital, left_y, tables.at[5], tables.at[3], out, *scratch, nothing, nothing)


def basic_tables(length):
    tables = []
    turn = (2, 3, 0, 1)
    flip = np.array([1.0, -1.0], np.float32)
    backward, forward = dft_pair(length, 1.0), dft_pair(length, -1.0)
    tables.append(table_halves(backward.transpose(turn)))
    tables.append(table_halves((backward * flip[:, None]).transpose(turn)))
    tables.append(table_halves(backward))
    tables.append(table_halves(forward.transpose(turn)))
    tables.append(table_halves((forward * flip[:, None, None, None]).transpose(turn)))
    tables.append(table_halves(forward))
    return tables


def whole_kernel(
    grids, resp_far, orbital_far, kernel_far, tables_far, weights, result_far, resp, orbital,
    kernel, tables, result, moved, part, got_half, half_sum, got_own, dens,
    away, here, back_away, back_here, out, in_away, in_here, out_away, out_here,
    pair_sent, pair_got, sent, got, in_sent, in_got, in_own, out_sent, out_got, out_own,
):
    devices = 4 * grids
    planes, length = part.shape[1], part.shape[2]
    own = planes // 4
    few = own // 2
    rows = length // devices
    block = 2 * own * rows
    band, grid = lax.axis_index("band"), lax.axis_index("grid")
    me = band * grids + grid

    def load(source, target, index):
        copy = pltpu.make_async_copy(source, target, moved.at[index])
        copy.start()
        return copy

    count = tables.shape[0]
    loads = [
        load(tables_far.at[pl.ds(0, 1)], tables.at[pl.ds(0, 1)], 0),
        load(resp_far.at[0], resp.at[0], 1),
        load(resp_far.at[1], resp.at[1], 2),
        load(tables_far.at[pl.ds(1, count - 1)], tables.at[pl.ds(1, count - 1)], 3),
        load(orbital_far, orbital, 4),
        load(kernel_far, kernel, 5),
    ]

    def before(stage):
        for copy in (loads[:2], loads[2:3], loads[3:])[stage]:
            copy.wait()

    stores = []

    def done(harmonic):
        stores.append(load(result.at[harmonic], result_far.at[harmonic], 6 + harmonic))

    def at(device):
        return {"band": device // grids, "grid": lax.rem(device, grids)}

    barrier = pltpu.get_barrier_semaphore()

    def greet(step, carry):
        pl.semaphore_signal(
            barrier, inc=1, device_id=at(lax.rem(me + step, devices)),
            device_id_type=pl.DeviceIdType.MESH,
        )
        return carry

    lax.fori_loop(1, devices, greet, 0)
    pl.semaphore_wait(barrier, devices - 1)

    low_bit, high_bit = lax.rem(band, 2), band // 2
    near = {"band": 2 * high_bit + (1 - low_bit), "grid": grid}
    far = {"band": 2 * (1 - high_bit) + low_bit, "grid": grid}

    def pair_copy(source, target, place, *index):
        return pltpu.make_async_remote_copy(
            src_ref=source, dst_ref=target, send_sem=pair_sent.at[index],
            recv_sem=pair_got.at[index], device_id=place, device_id_type=pl.DeviceIdType.MESH,
        )

    def add_bands(half):
        base = half * 2 * own
        kept = pl.ds(half * own, own)
        first = pair_copy(
            part.at[:, pl.ds(base + (1 - low_bit) * own, own)], got_half.at[:, kept], near, 0, half
        )
        first.start()
        first.wait()

        def add_half(plane, carry):
            for c in range(2):
                half_sum[c, half * own + plane] = (
                    part[c, base + low_bit * own + plane] + got_half[c, half * own + plane]
                )
            return carry

        lax.fori_loop(0, own, add_half, 0)
        second = pair_copy(
            half_sum.at[:, pl.ds(half * own + (1 - high_bit) * few, few)],
            got_own.at[:, pl.ds(half * few, few)], far, 1, half,
        )
        second.start()
        second.wait()
        for plane in range(few):
            for c in range(2):
                dens[c, half * few + plane] = (
                    half_sum[c, half * own + high_bit * few + plane]
                    + got_own[c, half * few + plane]
                )

    arrive(
        grids, resp, orbital, tables.at[0], tables.at[2], [tables.at[0], tables.at[1]], part,
        in_away, in_here, in_sent, in_got, in_own, add_bands, before,
    )

    def exchange(source, target, index):
        mine = pl.ds(pl.multiple_of(me * block, block), block)

        def copy_of(step):
            peer = lax.rem(me + step, devices)
            return pltpu.make_async_remote_copy(
                src_ref=source.at[pl.ds(pl.multiple_of(peer * block, block), block)],
                dst_ref=target.at[mine],
                send_sem=sent.at[index, step],
                recv_sem=got.at[index, step],
                device_id=at(peer),
                device_id_type=pl.DeviceIdType.MESH,
            )

        def start(step, carry):
            copy_of(step).start()
            return carry

        def finish(step, carry):
            copy_of(step).wait()
            return carry

        lax.fori_loop(1, devices, start, 0)
        target[mine, :] = source[mine, :]
        lax.fori_loop(1, devices, finish, 0)

    def lane(values, index):
        return values[:, index * length : (index + 1) * length]

    def beside(values):
        lines = [
            jnp.concatenate([lane(values, p)[:length], lane(values, p)[length:]], axis=1)
            for p in range(own)
        ]
        return jnp.concatenate(lines, axis=0)

    def spread(c, plane, row):
        return pl.ds((c * own + plane) * rows + row, devices, stride=block)

    field = jnp.concatenate(
        [jnp.concatenate([dens[c, p] for c in range(2)], axis=0) for p in range(own)], axis=1
    )
    wave = times_table(beside(table_times(tables.at[6], field)), tables.at[5])
    for p in range(own):
        for row in range(rows):
            top = p * length + row * devices
            for c in range(2):
                away[spread(c, p, row), :] = lane(wave[top : top + devices], c)
    exchange(away, here, 0)
    field = jnp.concatenate(
        [
            jnp.concatenate(
                [here[spread(c, p, row), :] for c in range(2) for p in range(own)], axis=0
            )
            for row in range(rows)
        ],
        axis=1,
    )
    wave = table_times(tables.at[7], field)
    weight = weights[...]
    wave = jnp.concatenate([wave[:length] * weight, wave[length:] * weight], axis=0)
    field = table_times(tables.at[8], wave)
    for row in range(rows):
        for c in range(2):
            for p in range(own):
                top = (c * own + p) * devices
                back_away[spread(c, p, row), :] = lane(field[top : top + devices], row)
    exchange(back_away, back_here, 1)
    wave = jnp.concatenate(
        [
            jnp.concatenate(
                [back_here[spread(c, p, row), :] for c in range(2) for row in range(rows)], axis=0
            )
            for p in range(own)
        ],
        axis=1,
    )
    cell = times_table(beside(table_times(tables.at[9], wave)), tables.at[2])
    third = []
    for half in range(2):
        low = half * 2 * own + low_bit * own + high_bit * few
        for q in range(few):
            p = half * few + q
            for c in range(2):
                value = lane(cell[p * length : (p + 1) * length], c)
                out[c, low + q] = value + kernel[low + q] * dens[c, p]
        mine = out.at[:, pl.ds(low, few)]
        third.append(pair_copy(mine, mine, far, 2, half))
        third[half].start()

    def gather(half):
        third[half].wait()
        mine = out.at[:, pl.ds(half * 2 * own + low_bit * own, own)]
        fourth = pair_copy(mine, mine, near, 3, half)
        fourth.start()
        fourth.wait()

    leave(
        grids, out, orbital, [tables.at[3], tables.at[4]], tables.at[5], tables.at[3], result,
        out_away, out_here, out_sent, out_got, out_own, gather, done,
    )
    for copy in stores:
        copy.wait()


def whole(grids, response, orbital, kernel_xc):
    planes, length = orbital.shape[0], orbital.shape[1]
    devices = 4 * grids
    own, rows = planes // 4, length // devices
    few = own // 2
    turn = (2, 3, 0, 1)
    kept = np.arange(rows)[:, None] + rows * np.arange(devices)[None, :]
    kept = kept.reshape(-1)
    place = np.array([0, 2, 1, 3])
    plane = np.arange(own)
    numbers = (
        (plane // few * 2 * own + plane % few)[:, None, None]
        + few * place[None, :, None]
        + planes * np.arange(grids)[None, None, :]
    ).reshape(-1)
    mine = (lax.axis_index("band") * grids + lax.axis_index("grid")) * rows
    freqs = signed_freq(jnp.arange(length, dtype=jnp.int32), length)
    own_freqs = signed_freq(mine + jnp.arange(rows, dtype=jnp.int32), length)
    weights = coulomb(freqs, own_freqs, freqs, length).reshape(length, rows * length)
    tables = basic_tables(length) + [
        table_halves(dft_pair(length, -1.0, columns=kept).transpose(turn)),
        table_halves(dft_pair(length, -1.0, rows=numbers).transpose(turn)),
        table_halves(dft_pair(length, 1.0, columns=numbers).transpose(turn)),
        table_halves(dft_pair(length, 1.0, rows=kept).transpose(turn)),
    ]
    operands = (response, orbital, kernel_xc, np.stack(tables), weights)

    def space(*shape):
        return pltpu.VMEM(shape, jnp.float32)

    parts = space(2 * own * length, length)
    flat = space(2, 2, length * planes, length)
    blocks = space(2, grids, 2, planes * planes, length)
    wide = space(2, planes, length, length)
    meets = pltpu.SemaphoreType.DMA((2, 2, grids))
    return pl.pallas_call(
        functools.partial(whole_kernel, grids),
        out_shape=jax.ShapeDtypeStruct(response.shape, jnp.float32),
        in_specs=[pl.BlockSpec(memory_space=pl.ANY)] * 4
        + [pl.BlockSpec(memory_space=pltpu.VMEM)],
        out_specs=pl.BlockSpec(memory_space=pl.ANY),
        scratch_shapes=[
            flat,
            space(planes, length, length),
            space(planes, length, length),
            pltpu.VMEM((len(tables), 2, 2 * length, 2 * length), jnp.bfloat16),
            flat,
            pltpu.SemaphoreType.DMA((8,)),
            wide,
            space(2, 2 * own, length, length),
            space(2, 2 * own, length, length),
            space(2, own, length, length),
            space(2, own, length, length),
            parts, parts, parts, parts,
            wide,
            flat, blocks, blocks, flat,
            pltpu.SemaphoreType.DMA((4, 2)),
            pltpu.SemaphoreType.DMA((4, 2)),
            pltpu.SemaphoreType.DMA((2, devices)),
            pltpu.SemaphoreType.DMA((2, devices)),
            meets, meets, pltpu.SemaphoreType.DMA((2, 2)),
            meets, meets, pltpu.SemaphoreType.DMA((2, 2)),
        ],
        compiler_params=pltpu.CompilerParams(
            collective_id=2, has_side_effects=True, vmem_limit_bytes=56 * 2**20
        ),
    )(*operands)


def call(kernel, grids, rows, length, out_shape, by_source, collective_id, *operands):
    flat = (2, 2, length * rows, length)
    blocks = (2, grids, 2, rows * rows, length)
    return pl.pallas_call(
        functools.partial(kernel, grids),
        out_shape=jax.ShapeDtypeStruct(out_shape, jnp.float32),
        in_specs=[pl.BlockSpec(memory_space=pltpu.VMEM)] * len(operands),
        out_specs=pl.BlockSpec(memory_space=pltpu.VMEM),
        scratch_shapes=[
            pltpu.VMEM(flat if by_source else blocks, jnp.float32),
            pltpu.VMEM(blocks if by_source else flat, jnp.float32),
            pltpu.SemaphoreType.DMA((2, 2, grids)),
            pltpu.SemaphoreType.DMA((2, 2, grids)),
            pltpu.SemaphoreType.DMA((2, 2)),
        ],
        compiler_params=pltpu.CompilerParams(
            collective_id=collective_id, has_side_effects=True, vmem_limit_bytes=40 * 2**20
        ),
    )(*operands)


def ein(form, operand, table):
    return jnp.einsum(form, operand, table, precision=high)


def signed_freq(positions, length):
    return jnp.where(positions < (length + 1) // 2, positions, positions - length).astype(
        jnp.float32
    )


def coulomb(freq_first, freq_second, freq_third, length):
    squares = (
        freq_first[:, None, None] ** 2
        + freq_second[None, :, None] ** 2
        + freq_third[None, None, :] ** 2
    )
    edge_len = spacing * length
    return jnp.where(
        squares > 0.5, edge_len * edge_len / (math.pi * jnp.maximum(squares, 1.0)), 0.0
    )


def hartree(density, axes, device, devices, numbers):
    length = density.shape[-1]
    forward, backward = dft_pair(length, -1.0), dft_pair(length, 1.0)
    wave = ein("cxyz,cydk->dxkz", density, forward)
    wave = ein("dxkz,dzem->exkm", wave, forward)
    wave = lax.all_to_all(wave, axes, split_axis=2, concat_axis=1, tiled=True)
    rows = length // devices
    mine = device * rows + jnp.arange(rows, dtype=jnp.int32)
    freqs = signed_freq(jnp.arange(length, dtype=jnp.int32), length)
    weights = coulomb(freqs, signed_freq(mine, length), freqs, length)
    wave = ein("cxyz,cxdk->dkyz", wave, dft_pair(length, -1.0, rows=numbers)) * weights
    wave = ein("dkyz,dkex->exyz", wave, dft_pair(length, 1.0, columns=numbers))
    wave = lax.all_to_all(wave, axes, split_axis=1, concat_axis=2, tiled=True)
    cell = ein("dxkz,dzem->exkm", wave, backward)
    return ein("cxyz,cydk->dxkz", cell, backward)


def on_device(bands, grids, ground, response, kernel_xc):
    grid_len = ground.shape[2]
    planes = ground.shape[1]
    orbital = ground[0]
    flat = response.reshape(2, 2, grid_len * planes, grid_len)
    if bands == 4 and planes % 8 == 0 and grid_len % (4 * grids) == 0:
        out = whole(grids, flat, orbital, kernel_xc)
    else:
        tables = np.stack(basic_tables(grid_len))
        partial = call(
            arrive_kernel, grids, planes, grid_len, (2, planes, grid_len, grid_len), True, 0,
            flat, orbital, tables,
        )
        dens = lax.psum(partial, "band")
        pot = hartree(dens, "grid", lax.axis_index("grid"), grids, None) + kernel_xc * dens
        out = call(
            leave_kernel, grids, planes, grid_len, (2, 2, grid_len * planes, grid_len), False, 1,
            pot, orbital, tables,
        )
    return out.reshape(1, 2, 2, grid_len, planes, grid_len)


def solution(mesh):
    bands, grids = mesh.shape["band"], mesh.shape["grid"]

    def body(ground, response, kernel_xc):
        return on_device(bands, grids, ground, response, kernel_xc)

    return jax.shard_map(
        body,
        mesh=mesh,
        in_specs=(
            P("band", "grid", None, None),
            P("band", None, None, None, "grid", None),
            P("grid", None, None),
        ),
        out_specs=P("band", None, None, None, "grid", None),
        check_vma=False,
    )
```
